512 devices in a mesh: fsdp: 2 (over core), prompt: 16 (over y, z_lo), resp: 16 (over z_hi, x).
Axes of the slice: x: 4, y: 4, z: 16 (z_hi: 4, z_lo: 4; z = z_hi * 4 + z_lo), core: 2. Of those that a mesh axis runs over, the one named last changes fastest.
Arguments:
- prompt_query: bfloat16 [256, 128, 4096], P(('prompt', 'resp'), None, 'fsdp'), may hold values from -250 to 250
- prompt_key: bfloat16 [256, 128, 512], P(('prompt', 'resp'), None, 'fsdp'), may hold values from -6 to 6
- prompt_value: bfloat16 [256, 128, 512], P(('prompt', 'resp'), None, 'fsdp'), may hold values from -6 to 6
- prompt_adapter: bfloat16 [256, 128, 128], P(('prompt', 'resp')), may hold values from -6 to 6
- prompt_upstream: bfloat16 [256, 128, 4096], P(('prompt', 'resp'), None, 'fsdp'), may hold values from -6 to 6
- answer_query: bfloat16 [256, 256, 4096], P(('prompt', 'resp'), None, 'fsdp'), may hold values from -250 to 250
- answer_key: bfloat16 [256, 256, 512], P(('prompt', 'resp'), None, 'fsdp'), may hold values from -6 to 6
- answer_value: bfloat16 [256, 256, 512], P(('prompt', 'resp'), None, 'fsdp'), may hold values from -6 to 6
- answer_adapter: bfloat16 [256, 256, 128], P(('prompt', 'resp')), may hold values from -6 to 6
- answer_upstream: bfloat16 [256, 256, 4096], P(('prompt', 'resp'), None, 'fsdp'), may hold values from -6 to 6
- adapter_up: bfloat16 [2, 64, 512], P(None, None, 'fsdp'), may hold values from -0.75 to 0.75
- lengths: int32 [256, 2], P(('prompt', 'resp')), may hold values from 1 to 128, as said below
- pairing: int32 [16, 16], P('prompt'), may hold values from 0 to 15, each once within a row
Outputs:
- prompt_adapter_grad: float32 [256, 128, 128], P(('prompt', 'resp'))
- answer_adapter_grad: float32 [256, 256, 128], P(('prompt', 'resp'))
- adapter_up_grad: float32 [2, 64, 512], P(None, None, 'fsdp')
The draws below stay inside these ranges and needn't reach their ends.
Inputs may be any that keep to these rules, and one draw needn't show every extreme that they name: Each row holds the lengths of one chosen and one rejected response; some length equals 128. `pairing`: each row is a permutation of the group's 16 indices.
All inputs are finite; a program needn't handle non-finite values.
Results may differ from the reference program's by a relative error of at most 0.02.
Values may be sent and summed in bfloat16 or wider, within the bound.
A program may use at most 64 MiB of HBM per device.

```python
import math
import jax
import jax.numpy as jnp
from jax import lax

QH = 32
KVH = 4
HD = 128
RANK = 64
PLEN = 128
MOST = 128
SLOTS = 256
PROMPTS = 256
N_PROMPT = 16
N_RESP = 16


def draw_prompt_query(key, part):
    key = jax.random.fold_in(key, 3)
    base_key = jax.random.fold_in(key, 0)
    values = jax.random.normal(base_key, (PROMPTS, PLEN, QH * HD), jnp.float32)
    return jnp.clip(values, -250.0, 250.0).astype(jnp.bfloat16)


def draw_answer_query(key, part):
    key = jax.random.fold_in(key, 5)
    base_key = jax.random.fold_in(key, 0)
    values = jax.random.normal(base_key, (PROMPTS, SLOTS, QH * HD), jnp.float32)
    return jnp.clip(values, -250.0, 250.0).astype(jnp.bfloat16)


def draw_lengths(key, part):
    key = jax.random.fold_in(key, 11)
    first_key, second_key = jax.random.split(key)
    drawn = jax.random.randint(first_key, (PROMPTS * 2,), 1, MOST + 1)
    chosen_spot = jax.random.randint(second_key, (), 0, PROMPTS * 2)
    filled = jnp.where(jnp.arange(PROMPTS * 2) == chosen_spot, MOST, drawn)
    return filled.reshape(PROMPTS, 2).astype(jnp.int32)


def steps_of(rng, extent, cuts, least, high):
    def one(axis_at, parts):
        heights = jax.random.uniform(jax.random.fold_in(jax.random.fold_in(rng, 6), axis_at), (parts,), jnp.float32, least / len(cuts), high / len(cuts))
        return jnp.repeat(jnp.exp(heights), extent[axis_at] // parts).reshape((-1,) + (1,) * (len(extent) - axis_at - 1))

    loudness = one(*cuts[0])
    for cut in cuts[1:]:
        loudness = loudness * one(*cut)
    return loudness


def centred(key, shape, spread, reach, cuts=(), held_as=jnp.bfloat16):
    loudness = steps_of(key, shape, cuts, -0.22, 0.18) if cuts else 1.0
    values = jax.random.normal(key, shape, jnp.float32) * spread * loudness
    return jnp.minimum(jnp.maximum(values, -reach), reach).astype(held_as)


def setup_inputs(seed: int = 0) -> dict:
    keys = jax.random.split(jax.random.key(seed), 14)
    return {
        "prompt_query": draw_prompt_query(jax.random.fold_in(keys[13], 71), 0),
        "prompt_key": centred(keys[1], (PROMPTS, PLEN, KVH * HD), 1.0, 6.0, ((0, 256), (2, 2))),
        "prompt_value": centred(keys[2], (PROMPTS, PLEN, KVH * HD), 1.0, 6.0, ((0, 256), (2, 2))),
        "prompt_adapter": centred(keys[3], (PROMPTS, PLEN, 2 * RANK), 1.0, 6.0, ((0, 256),)),
        "prompt_upstream": centred(keys[4], (PROMPTS, PLEN, QH * HD), 1.0, 6.0, ((0, 256), (2, 2))),
        "answer_query": draw_answer_query(jax.random.fold_in(keys[13], 71), 0),
        "answer_key": centred(keys[6], (PROMPTS, SLOTS, KVH * HD), 1.0, 6.0, ((0, 256), (2, 2))),
        "answer_value": centred(keys[7], (PROMPTS, SLOTS, KVH * HD), 1.0, 6.0, ((0, 256), (2, 2))),
        "answer_adapter": centred(keys[8], (PROMPTS, SLOTS, 2 * RANK), 1.0, 6.0, ((0, 256),)),
        "answer_upstream": centred(keys[9], (PROMPTS, SLOTS, QH * HD), 1.0, 6.0, ((0, 256), (2, 2))),
        "adapter_up": centred(keys[10], (2, RANK, KVH * HD), RANK ** -0.5, 0.75, ((2, 2),)),
        "lengths": draw_lengths(jax.random.fold_in(keys[13], 71), 0),
        "pairing": jax.vmap(lambda own: jax.random.permutation(own, N_RESP))(jax.random.split(keys[12], N_PROMPT)).reshape((N_PROMPT, N_RESP)).astype(jnp.int32),
    }


exact_mode = lax.Precision.HIGHEST

def full_projection(base_rows, adapter_in, adapter_out):
    lifted = jnp.dot(adapter_in, adapter_out, preferred_element_type=jnp.float32)
    return (base_rows.astype(jnp.float32) + lifted).astype(jnp.bfloat16)

def attend_back(queries, key_rows, value_rows, upstream, visible):
    query_count = queries.shape[0]
    key_count = key_rows.shape[0]
    factor = 1.0 / math.sqrt(HD)
    query_heads = queries.astype(jnp.float32).reshape(query_count, KVH, QH // KVH, HD)
    key_heads = key_rows.astype(jnp.float32).reshape(key_count, KVH, HD)
    value_heads = value_rows.astype(jnp.float32).reshape(key_count, KVH, HD)
    grad_heads = upstream.astype(jnp.float32).reshape(query_count, KVH, QH // KVH, HD)
    scores = jnp.einsum('rkgd,ckd->kgrc', query_heads, key_heads) * factor
    scores = jnp.where(visible, scores, -1e+30)
    highest = lax.optimization_barrier(jnp.max(scores, axis=-1, keepdims=True))
    weights = jnp.exp(scores - highest)
    probs_full = weights / lax.optimization_barrier(jnp.sum(weights, axis=-1, keepdims=True))
    probs_wide = lax.optimization_barrier(probs_full.astype(jnp.bfloat16)).astype(jnp.float32)
    output = jnp.einsum('kgrc,ckd->rkgd', probs_wide, value_heads)
    row_delta = lax.optimization_barrier(jnp.sum(grad_heads * output, axis=-1))
    dprobs = jnp.einsum('rkgd,ckd->kgrc', grad_heads, value_heads)
    dscores = probs_full * (dprobs - jnp.transpose(row_delta, (1, 2, 0))[..., None])
    dscores_wide = lax.optimization_barrier(dscores.astype(jnp.bfloat16)).astype(jnp.float32)
    key_grads = jnp.einsum('kgrc,rkgd->ckd', dscores_wide, query_heads) * factor
    value_grads = jnp.einsum('kgrc,rkgd->ckd', probs_wide, grad_heads)
    return (key_grads.reshape(key_count, KVH * HD), value_grads.reshape(key_count, KVH * HD))

def reference(prompt_query, prompt_key, prompt_value, prompt_adapter, prompt_upstream, answer_query, answer_key, answer_value, answer_adapter, answer_upstream, adapter_up, lengths, pairing):
    prompt_keys = full_projection(prompt_key, prompt_adapter[:, :, :RANK], adapter_up[0])
    prompt_values = full_projection(prompt_value, prompt_adapter[:, :, RANK:], adapter_up[1])
    answer_keys = full_projection(answer_key, answer_adapter[:, :, :RANK], adapter_up[0])
    answer_values = full_projection(answer_value, answer_adapter[:, :, RANK:], adapter_up[1])
    slot_index = jnp.arange(SLOTS, dtype=jnp.int32)
    part_index = slot_index // MOST
    place_index = slot_index % MOST
    live_mask = place_index[None, :] < jnp.where(part_index[None, :] == 0, lengths[:, :1], lengths[:, 1:])
    answer_grad_in = answer_upstream * live_mask[:, :, None].astype(jnp.bfloat16)
    positions = jnp.arange(PLEN, dtype=jnp.int32)
    causal = positions[None, :] <= positions[:, None]
    same_part = (part_index[:, None] == part_index[None, :]) & (place_index[None, :] <= place_index[:, None])
    answer_visible = jnp.concatenate([jnp.ones((SLOTS, PLEN), dtype=bool), same_part], axis=1)
    owners = jnp.arange(PROMPTS, dtype=jnp.int32) // N_RESP * N_RESP + pairing.reshape(-1).astype(jnp.int32)

    def one_row(row_index):
        own_key_grad, own_value_grad = attend_back(prompt_query[row_index], prompt_keys[row_index], prompt_values[row_index], prompt_upstream[row_index], causal)
        source = owners[row_index]
        key_rows = jnp.concatenate([prompt_keys[source], answer_keys[row_index]], axis=0)
        value_rows = jnp.concatenate([prompt_values[source], answer_values[row_index]], axis=0)
        all_key_grad, all_value_grad = attend_back(answer_query[row_index], key_rows, value_rows, answer_grad_in[row_index], answer_visible)
        return (own_key_grad, own_value_grad, all_key_grad[:PLEN], all_value_grad[:PLEN], all_key_grad[PLEN:], all_value_grad[PLEN:])
    results = lax.map(one_row, jnp.arange(PROMPTS, dtype=jnp.int32))
    own_key_grad, own_value_grad, prefix_key_grad, prefix_value_grad, slot_key_grad, slot_value_grad = results
    prompt_key_grad = own_key_grad + jnp.zeros_like(own_key_grad).at[owners].add(prefix_key_grad)
    prompt_value_grad = own_value_grad + jnp.zeros_like(own_value_grad).at[owners].add(prefix_value_grad)
    up_keys = adapter_up[0].astype(jnp.float32)
    up_values = adapter_up[1].astype(jnp.float32)

    def project(key_grad, value_grad):
        key_part = jnp.einsum('prw,cw->prc', key_grad, up_keys, precision=exact_mode)
        value_part = jnp.einsum('prw,cw->prc', value_grad, up_values, precision=exact_mode)
        return jnp.concatenate([key_part, value_part], axis=-1)
    prompt_adapter_grad = project(prompt_key_grad, prompt_value_grad)
    answer_adapter_grad = project(slot_key_grad, slot_value_grad)

    def outer(adapter_in, key_grad, value_grad):
        inputs_wide = adapter_in.astype(jnp.float32)
        key_part = jnp.einsum('prc,prw->cw', inputs_wide[:, :, :RANK], key_grad, precision=exact_mode)
        value_part = jnp.einsum('prc,prw->cw', inputs_wide[:, :, RANK:], value_grad, precision=exact_mode)
        return jnp.stack([key_part, value_part])
    grad_total = outer(prompt_adapter, prompt_key_grad, prompt_value_grad) + outer(answer_adapter, slot_key_grad, slot_value_grad)
    adapter_up_grad = grad_total / math.sqrt(PROMPTS * (PLEN + MOST))
    return (prompt_adapter_grad, answer_adapter_grad, adapter_up_grad)
```

```python
import functools
import math

import jax
import jax.numpy as jnp
from jax import lax
from jax.experimental import pallas as pl
from jax.experimental.pallas import tpu as pltpu
from jax.sharding import PartitionSpec as P

MESH = pl.DeviceIdType.MESH
HD = 128
T = 128
N = 16
NT = (((1,), (1,)), ((), ()))
TN = (((0,), (0,)), ((), ()))
NN = (((1,), (0,)), ((), ()))
FACTOR = 1.0 / math.sqrt(HD)
EXP2_FACTOR = FACTOR * math.log2(math.e)


def mm(a, b, dims):
    return lax.dot_general(a, b, dims, preferred_element_type=jnp.float32)


def ready(ref, sem):
    pltpu.make_async_copy(ref, ref, sem).wait()


def backward_tile(keys, values, queries, grads, visible, live, prefix):
    scores = mm(keys, queries, NT)
    dprobs = mm(values, grads, NT)
    own = jnp.where(visible, scores[prefix:], -1e30)
    highest = jnp.max(own, axis=0, keepdims=True)
    if prefix:
        highest = jnp.maximum(highest, jnp.max(scores[:prefix], axis=0, keepdims=True))
        scores = jnp.concatenate([scores[:prefix], own], axis=0)
    else:
        scores = own
    weights = jnp.exp2((scores - highest) * EXP2_FACTOR)
    inverse = 1.0 / jnp.sum(weights, axis=0, keepdims=True)
    if live is not None:
        inverse = jnp.where(live, inverse, 0.0)
    probs = weights * inverse
    delta = jnp.sum(probs * dprobs, axis=0, keepdims=True)
    dscores = probs * (dprobs - delta)
    return probs.astype(jnp.bfloat16), dscores.astype(jnp.bfloat16)


def kernel(
    scale,
    pq_h, pk_h, pv_h, pa_h, pg_h, aq_h, ak_h, av_h, aa_h, ag_h, up_h, lens, pairing,
    prompt_out, answer_out, up_out,
    pq, pk, pv, pa, pg, aq, ak, av, aa, ag, up,
    wide_up, kv_own, kv_slot, kv_pre, mid1, mid2, amid1, amid2, a_pre,
    probs_s, dsc_s, dkv, own_proj, outer_acc,
    pre_send, bmid1, bmid2, pre_recv, pr_send, pr_recv, an_send, an_recv,
    gr_send, gr1, gr2_send, gr2, gr3_send, gr3,
    load_sem, send_sem, recv_sem,
):
    f = lax.axis_index("fsdp")
    p = lax.axis_index("prompt")
    r = lax.axis_index("resp")
    twin = 1 - f
    is_mid = lax.rem(r, 2) == f
    tile_at = r // 2

    loads = [
        pltpu.make_async_copy(src.at[0] if lead else src, dst, load_sem.at[i])
        for i, (src, dst, lead) in enumerate([
            (up_h, up, False), (pa_h, pa, True), (pk_h, pk, True), (pv_h, pv, True),
            (pq_h, pq, True), (pg_h, pg, True), (aa_h, aa, True), (ak_h, ak, True),
            (av_h, av, True), (aq_h, aq, True), (ag_h, ag, True),
        ])
    ]
    for load in loads:
        load.start()

    barrier = pltpu.get_barrier_semaphore()
    pl.semaphore_signal(barrier, inc=1, device_id={"fsdp": twin}, device_id_type=MESH)

    def greet(k, carry):
        pl.semaphore_signal(barrier, inc=1, device_id={"resp": lax.rem(r + k, N)}, device_id_type=MESH)
        pl.semaphore_signal(barrier, inc=1, device_id={"prompt": lax.rem(p + k, N)}, device_id_type=MESH)
        return carry

    lax.fori_loop(1, N, greet, 0)

    wide_up[...] = jnp.zeros_like(wide_up)
    for load in loads[:4]:
        load.wait()
    wide_up[0:64, 0:256] = up[0]
    wide_up[64:128, 256:512] = up[1]
    lifted = mm(pa[...], wide_up[...], NN)
    kv_own[0:128, :] = (pk[...].astype(jnp.float32) + lifted[:, 0:256]).astype(jnp.bfloat16)
    kv_own[128:256, :] = (pv[...].astype(jnp.float32) + lifted[:, 256:512]).astype(jnp.bfloat16)

    pl.semaphore_wait(barrier, 2 * (N - 1) + 1)

    def to(src, dst, lane, where):
        return pltpu.make_async_remote_copy(
            src_ref=src, dst_ref=dst, send_sem=send_sem.at[lane], recv_sem=recv_sem.at[lane],
            device_id=where, device_id_type=MESH,
        )

    def rows(index):
        return pl.ds(pl.multiple_of(index * 16, 16), 16)

    def to_mids(src_of, dst, lane):
        @pl.when(is_mid)
        def _():
            def step(k, carry):
                peer = lax.rem(r + 2 * k + 2, N)
                to(src_of(peer // 2), dst.at[r], lane, {"resp": peer}).start()
                return carry

            lax.fori_loop(0, 7, step, 0)
            dst[r] = src_of(tile_at)[...]

        @pl.when(jnp.logical_not(is_mid))
        def _():
            def step(k, carry):
                peer = lax.rem(r + 2 * k + 1, N)
                to(src_of(peer // 2), dst.at[r], lane, {"resp": peer}).start()
                return carry

            lax.fori_loop(0, 8, step, 0)

    def mids_sent(ref, lane):
        @pl.when(is_mid)
        def _():
            pltpu.make_async_copy(ref.at[pl.ds(0, 7)], ref.at[pl.ds(0, 7)], send_sem.at[lane]).wait()

        @pl.when(jnp.logical_not(is_mid))
        def _():
            pltpu.make_async_copy(ref.at[pl.ds(0, 8)], ref.at[pl.ds(0, 8)], send_sem.at[lane]).wait()

    def forward(k, carry):
        peer = lax.rem(r + k, N)
        to(kv_own.at[rows(peer)], mid1.at[r], 0, {"resp": peer}).start()
        return carry

    lax.fori_loop(1, N, forward, 0)
    mid1[r] = kv_own[rows(r), :]
    to_mids(lambda t: pa.at[rows(t)], amid1, 1)

    lane_at = lax.rem(lax.broadcasted_iota(jnp.int32, (T, 256), 1), T)
    visible = lax.broadcasted_iota(jnp.int32, (T, 256), 0) <= lane_at
    loads[4].wait()
    loads[5].wait()

    def own_head(h, carry):
        at = pl.multiple_of(h * HD, HD)
        keys = kv_own[0:128, pl.ds(at, HD)]
        values = kv_own[128:256, pl.ds(at, HD)]

        def heads(ref, g, count):
            return jnp.concatenate(
                [ref[:, pl.ds(pl.multiple_of(h * 1024 + (g + i) * HD, HD), HD)] for i in range(count)], axis=0
            )

        for g in range(0, 8, 2):
            probs, dscores = backward_tile(keys, values, heads(pq, g, 2), heads(pg, g, 2), visible, None, 0)
            probs_s[0, 0:128, g * HD:(g + 2) * HD] = probs
            dsc_s[0, 0:128, g * HD:(g + 2) * HD] = dscores
        dkv[0:128, pl.ds(at, HD)] = (mm(dsc_s[0, 0:128, :], heads(pq, 0, 8), NN) * FACTOR).astype(jnp.bfloat16)
        dkv[0:128, pl.ds(pl.multiple_of(256 + h * HD, HD), HD)] = mm(
            probs_s[0, 0:128, :], heads(pg, 0, 8), NN
        ).astype(jnp.bfloat16)
        return carry

    lax.fori_loop(0, 2, own_head, 0)

    ready(mid1.at[pl.ds(0, 15)], recv_sem.at[0])

    def onward(k, carry):
        peer = lax.rem(r + k, N)
        mid2[peer] = mid1[pairing[0, peer]]
        to(mid2.at[peer], kv_pre.at[rows(r)], 2, {"resp": peer}).start()
        return carry

    lax.fori_loop(1, N, onward, 0)
    kv_pre[rows(r), :] = mid1[pairing[0, r]]

    @pl.when(is_mid)
    def _():
        ready(amid1.at[pl.ds(0, 15)], recv_sem.at[1])

        def step(k, carry):
            peer = lax.rem(r + k, N)
            amid2[peer] = amid1[pairing[0, peer]]
            to(amid2.at[peer], a_pre.at[rows(tile_at)], 3, {"resp": peer}).start()
            return carry

        lax.fori_loop(1, N, step, 0)
        a_pre[rows(tile_at), :] = amid1[pairing[0, r]]

    own_proj[...] = mm(dkv[0:128, :], wide_up[...], NT)
    for load in loads[6:]:
        load.wait()
    lifted_slots = mm(aa[...], wide_up[...], NN)
    kv_slot[:, 0:256] = (ak[...].astype(jnp.float32) + lifted_slots[:, 0:256]).astype(jnp.bfloat16)
    kv_slot[:, 256:512] = (av[...].astype(jnp.float32) + lifted_slots[:, 256:512]).astype(jnp.bfloat16)
    outer_acc[...] = mm(pa[...], dkv[0:128, :], TN)

    ready(kv_pre.at[pl.ds(0, 240)], recv_sem.at[2])
    row_at = lax.rem(lax.broadcasted_iota(jnp.int32, (1, 256), 1), T)

    def slot_head(h, carry):
        at = pl.multiple_of(h * HD, HD)
        value_at = pl.multiple_of(256 + h * HD, HD)
        key_sum, value_sum = 0.0, 0.0
        for c in range(2):
            part = slice(c * T, (c + 1) * T)
            keys = jnp.concatenate([kv_pre[0:128, pl.ds(at, HD)], kv_slot[part, pl.ds(at, HD)]], axis=0)
            values = jnp.concatenate([kv_pre[128:256, pl.ds(at, HD)], kv_slot[part, pl.ds(value_at, HD)]], axis=0)
            live = row_at < lens[0, c]

            def heads(ref, g, count):
                return jnp.concatenate(
                    [ref[part, pl.ds(pl.multiple_of(h * 1024 + (g + i) * HD, HD), HD)] for i in range(count)], axis=0
                )

            for g in range(0, 8, 2):
                probs, dscores = backward_tile(keys, values, heads(aq, g, 2), heads(ag, g, 2), visible, live, T)
                probs_s[c, :, g * HD:(g + 2) * HD] = probs
                dsc_s[c, :, g * HD:(g + 2) * HD] = dscores
            key_grad = mm(dsc_s[c], heads(aq, 0, 8), NN) * FACTOR
            value_grad = mm(probs_s[c], heads(ag, 0, 8), NN)
            dkv[256 + c * T:256 + (c + 1) * T, pl.ds(at, HD)] = key_grad[T:].astype(jnp.bfloat16)
            dkv[256 + c * T:256 + (c + 1) * T, pl.ds(value_at, HD)] = value_grad[T:].astype(jnp.bfloat16)
            key_sum = key_sum + key_grad[:T]
            value_sum = value_sum + value_grad[:T]
        dkv[128:256, pl.ds(at, HD)] = key_sum.astype(jnp.bfloat16)
        dkv[128:256, pl.ds(value_at, HD)] = value_sum.astype(jnp.bfloat16)
        return carry

    lax.fori_loop(0, 2, slot_head, 0)

    pre_send[...] = mm(dkv[128:256, :], wide_up[...], NT).astype(jnp.bfloat16).reshape(8, 16, 128)
    to_mids(lambda t: pre_send.at[t], bmid1, 4)

    @pl.when(is_mid)
    def _():
        ready(a_pre.at[pl.ds(0, 112)], recv_sem.at[3])

    @pl.when(jnp.logical_not(is_mid))
    def _():
        ready(a_pre, recv_sem.at[3])

    outer = outer_acc[...] + mm(a_pre[...], dkv[128:256, :], TN) + mm(aa[...], dkv[256:512, :], TN)
    for b, (row, col) in enumerate([(0, 0), (0, 128), (64, 256), (64, 384)]):
        gr_send[4 * b:4 * b + 4] = outer[row:row + 64, col:col + 128].astype(jnp.bfloat16).reshape(4, 16, 128)

    def scatter(k, carry):
        peer = lax.rem(p + k, N)
        to(gr_send.at[peer], gr1.at[p], 5, {"prompt": peer}).start()
        return carry

    lax.fori_loop(1, N, scatter, 0)
    gr1[p] = gr_send[p]

    an_send[...] = mm(dkv[256:512, :], wide_up[...], NT).astype(jnp.bfloat16)
    to_twin = to(an_send, an_recv, 6, {"fsdp": twin})
    to_twin.start()

    @pl.when(is_mid)
    def _():
        ready(bmid1.at[pl.ds(0, 15)], recv_sem.at[4])

        def step(k, carry):
            peer = lax.rem(r + k, N)
            held = jnp.int32(0)
            for d in range(N):
                held = jnp.where(pairing[0, d] == peer, d, held)
            bmid2[peer] = bmid1[held]
            to(bmid2.at[peer], pre_recv.at[tile_at], 7, {"resp": peer}).start()
            return carry

        lax.fori_loop(1, N, step, 0)
        held = jnp.int32(0)
        for d in range(N):
            held = jnp.where(pairing[0, d] == r, d, held)
        pre_recv[tile_at] = bmid1[held]

    ready(gr1.at[pl.ds(0, 15)], recv_sem.at[5])
    part_sum = jnp.sum(gr1[...].astype(jnp.float32), axis=0).astype(jnp.bfloat16)
    gr2_send[...] = part_sum

    def spread(k, carry):
        peer = lax.rem(r + k, N)
        to(gr2_send, gr2.at[r], 8, {"resp": peer}).start()
        return carry

    lax.fori_loop(1, N, spread, 0)
    gr2[r] = part_sum

    to_twin.wait_recv()
    answer_out[0] = an_send[...].astype(jnp.float32) + an_recv[...].astype(jnp.float32)

    @pl.when(is_mid)
    def _():
        ready(pre_recv.at[pl.ds(0, 7)], recv_sem.at[7])

    @pl.when(jnp.logical_not(is_mid))
    def _():
        ready(pre_recv, recv_sem.at[7])

    pr_send[...] = (own_proj[...] + pre_recv[...].reshape(128, 128).astype(jnp.float32)).astype(jnp.bfloat16)
    prompt_twin = to(pr_send, pr_recv, 9, {"fsdp": twin})
    prompt_twin.start()

    ready(gr2.at[pl.ds(0, 15)], recv_sem.at[8])
    total = (jnp.sum(gr2[...].astype(jnp.float32), axis=0) * scale).astype(jnp.bfloat16)
    gr3_send[...] = total

    def collect(k, carry):
        peer = lax.rem(p + k, N)
        to(gr3_send, gr3.at[p], 10, {"prompt": peer}).start()
        return carry

    lax.fori_loop(1, N, collect, 0)
    gr3[p] = total

    prompt_twin.wait_recv()
    prompt_out[0] = pr_send[...].astype(jnp.float32) + pr_recv[...].astype(jnp.float32)

    ready(gr3.at[pl.ds(0, 15)], recv_sem.at[10])
    for b in range(4):
        up_out[b // 2, :, (b % 2) * 128:(b % 2) * 128 + 128] = (
            gr3[4 * b:4 * b + 4].reshape(64, 128).astype(jnp.float32)
        )

    ready(mid1.at[pl.ds(0, 15)], send_sem.at[0])
    mids_sent(amid1, 1)
    ready(mid2.at[pl.ds(0, 15)], send_sem.at[2])
    mids_sent(bmid1, 4)
    ready(gr_send.at[pl.ds(0, 15)], send_sem.at[5])
    to_twin.wait_send()
    ready(gr2.at[pl.ds(0, 15)], send_sem.at[8])
    prompt_twin.wait_send()
    ready(gr3.at[pl.ds(0, 15)], send_sem.at[10])

    @pl.when(is_mid)
    def _():
        ready(amid2.at[pl.ds(0, 15)], send_sem.at[3])
        ready(bmid2.at[pl.ds(0, 15)], send_sem.at[7])


def on_device(scale, *args):
    bf, f32 = jnp.bfloat16, jnp.float32
    hbm = pl.BlockSpec(memory_space=pl.ANY)
    vmem = pl.BlockSpec(memory_space=pltpu.VMEM)
    smem = pl.BlockSpec(memory_space=pltpu.SMEM)
    V = pltpu.VMEM
    return pl.pallas_call(
        functools.partial(kernel, scale),
        out_shape=(
            jax.ShapeDtypeStruct((1, 128, 128), f32),
            jax.ShapeDtypeStruct((1, 256, 128), f32),
            jax.ShapeDtypeStruct((2, 64, 256), f32),
        ),
        in_specs=[hbm] * 11 + [smem] * 2,
        out_specs=(vmem, vmem, vmem),
        scratch_shapes=[
            V((128, 2048), bf), V((128, 256), bf), V((128, 256), bf), V((128, 128), bf), V((128, 2048), bf),
            V((256, 2048), bf), V((256, 256), bf), V((256, 256), bf), V((256, 128), bf), V((256, 2048), bf),
            V((2, 64, 256), bf),
            V((128, 512), bf), V((256, 256), bf), V((256, 512), bf), V((256, 256), bf),
            V((16, 16, 256), bf), V((16, 16, 256), bf), V((16, 16, 128), bf), V((16, 16, 128), bf), V((128, 128), bf),
            V((2, 256, 1024), bf), V((2, 256, 1024), bf), V((512, 512), bf), V((128, 128), f32), V((128, 512), f32),
            V((8, 16, 128), bf), V((16, 16, 128), bf), V((16, 16, 128), bf), V((8, 16, 128), bf),
            V((128, 128), bf), V((128, 128), bf), V((256, 128), bf), V((256, 128), bf),
            V((16, 16, 128), bf), V((16, 16, 128), bf), V((16, 128), bf), V((16, 16, 128), bf),
            V((16, 128), bf), V((16, 16, 128), bf),
            pltpu.SemaphoreType.DMA((11,)), pltpu.SemaphoreType.DMA((11,)), pltpu.SemaphoreType.DMA((11,)),
        ],
        compiler_params=pltpu.CompilerParams(
            collective_id=0, has_side_effects=True, vmem_limit_bytes=48 * 1024 * 1024
        ),
        name="adapter_backward",
    )(*args)


def solution(mesh):
    rows = ("prompt", "resp")
    wide = P(rows, None, "fsdp")
    whole = P(rows, None, None)
    scale = 1.0 / math.sqrt(mesh.shape["prompt"] * mesh.shape["resp"] * 2 * T)
    return jax.shard_map(
        functools.partial(on_device, scale),
        mesh=mesh,
        in_specs=(
            wide, wide, wide, whole, wide, wide, wide, wide, whole, wide,
            P(None, None, "fsdp"), P(rows, None), P("prompt", None),
        ),
        out_specs=(whole, whole, P(None, None, "fsdp")),
        check_vma=False,
    )
```

```python
import functools
import math

import jax
import jax.numpy as jnp
from jax import lax
from jax.experimental import pallas as pl
from jax.experimental.pallas import tpu as pltpu
from jax.sharding import PartitionSpec as P

MESH = pl.DeviceIdType.MESH
HD = 128
T = 128
N = 16
NT = (((1,), (1,)), ((), ()))
TN = (((0,), (0,)), ((), ()))
NN = (((1,), (0,)), ((), ()))
FACTOR = 1.0 / math.sqrt(HD)
EXP2_FACTOR = FACTOR * math.log2(math.e)
RESP_ORDER = (10, 9, 11, 8, 6, 14, 5, 7, 13, 15, 4, 12, 2, 1, 3)
PLANE_ORDER = (10, 9, 11, 6, 14, 8, 2, 5, 7, 13, 15, 4, 12, 1, 3)
RING_ORDER = (8, 7, 9, 6, 10, 5, 11, 4, 12, 3, 13, 2, 14, 1, 15)


def mm(a, b, dims):
    return lax.dot_general(a, b, dims, preferred_element_type=jnp.float32)


def ready(ref, sem):
    pltpu.make_async_copy(ref, ref, sem).wait()


def backward_tile(keys, values, queries, grads, visible, live, prefix):
    scores = mm(keys, queries, NT)
    dprobs = mm(values, grads, NT)
    own = jnp.where(visible, scores[prefix:], -1e30)
    highest = jnp.max(own, axis=0, keepdims=True)
    if prefix:
        highest = jnp.maximum(highest, jnp.max(scores[:prefix], axis=0, keepdims=True))
        scores = jnp.concatenate([scores[:prefix], own], axis=0)
    else:
        scores = own
    weights = jnp.exp2((scores - highest) * EXP2_FACTOR)
    inverse = 1.0 / jnp.sum(weights, axis=0, keepdims=True)
    if live is not None:
        inverse = jnp.where(live, inverse, 0.0)
    probs = weights * inverse
    delta = jnp.sum(probs * dprobs, axis=0, keepdims=True)
    dscores = probs * (dprobs - delta)
    return probs.astype(jnp.bfloat16), dscores.astype(jnp.bfloat16)


def kernel(
    scale,
    pq_h, pk_h, pv_h, pa_h, pg_h, aq_h, ak_h, av_h, aa_h, ag_h, up_h, lens_h, pairing_h,
    prompt_out, answer_out, up_out,
    pq, pk, pv, pa, pg, aq, ak, av, aa, ag, up, lens, pairing,
    wide_up, kv_own, kv_slot, kv_pre, mid1, mid2, amid1, amid2, a_pre,
    probs_s, dsc_s, dkv, own_proj, outer_acc,
    own_half, own_twin, pre_part, pre_twin, pre_half, pre_x, pre_z, pre_pick, pre_home, done_half, done_twin,
    an_send, an_recv, gr_send, gr1, gr2_send, gr2, gr3_send, gr3,
    load_sem, send_sem, recv_sem,
):
    f = lax.axis_index("fsdp")
    p = lax.axis_index("prompt")
    r = lax.axis_index("resp")
    twin = {"fsdp": 1 - f}
    x, z_hi = lax.rem(r, 4), r // 4
    y, z_lo = p // 4, lax.rem(p, 4)
    is_mid = lax.rem(r, 4) == 2 * f
    plane = y * 4 + x
    ring = z_hi * 4 + z_lo

    def in_plane(at):
        return {"prompt": (at // 4) * 4 + z_lo, "resp": z_hi * 4 + lax.rem(at, 4)}

    def in_ring(at):
        return {"prompt": y * 4 + lax.rem(at, 4), "resp": (at // 4) * 4 + x}

    def along_x(k):
        return z_hi * 4 + lax.rem(x + k, 4)

    def along_z(k):
        return lax.rem(z_hi + k, 4) * 4 + x

    barrier = pltpu.get_barrier_semaphore()

    def greet(where):
        pl.semaphore_signal(barrier, inc=1, device_id=where, device_id_type=MESH)

    for k in RESP_ORDER:
        greet({"resp": lax.rem(r + k, N)})

    loads = [
        pltpu.make_async_copy(src.at[0] if lead else src, dst, load_sem.at[i])
        for i, (src, dst, lead) in enumerate([
            (up_h, up, False), (pa_h, pa, True), (pk_h, pk, True), (pv_h, pv, True),
            (pq_h, pq, True), (pg_h, pg, True), (aa_h, aa, True), (ak_h, ak, True),
            (av_h, av, True), (aq_h, aq, True), (ag_h, ag, True), (lens_h, lens, False), (pairing_h, pairing, False),
        ])
    ]
    for load in loads:
        load.start()

    greet(twin)
    for k in range(4, N):
        greet({"prompt": (lax.rem(y + k // 4, 4)) * 4 + z_lo, "resp": along_x(k % 4)})
    for k in range(4, N):
        greet({"prompt": y * 4 + lax.rem(z_lo + k // 4, 4), "resp": along_z(k % 4)})

    wide_up[...] = jnp.zeros_like(wide_up)
    for load in loads[:4]:
        load.wait()
    wide_up[0:64, 0:256] = up[0]
    wide_up[64:128, 256:512] = up[1]
    lifted = mm(pa[...], wide_up[...], NN)
    kv_own[0:128, :] = (pk[...].astype(jnp.float32) + lifted[:, 0:256]).astype(jnp.bfloat16)
    kv_own[128:256, :] = (pv[...].astype(jnp.float32) + lifted[:, 256:512]).astype(jnp.bfloat16)

    pl.semaphore_wait(barrier, 40)

    def to(src, dst, lane, where):
        return pltpu.make_async_remote_copy(
            src_ref=src, dst_ref=dst, send_sem=send_sem.at[lane], recv_sem=recv_sem.at[lane],
            device_id=where, device_id_type=MESH,
        )

    def rows(index, size=16):
        return pl.ds(pl.multiple_of(index * size, size), size)

    for k in RESP_ORDER:
        peer = lax.rem(r + k, N)
        to(kv_own.at[rows(peer)], mid1.at[r], 0, {"resp": peer}).start()
    mid1[r] = kv_own[rows(r), :]
    for i in range(4):
        member = 4 * i + 2 * f

        @pl.when(member != r)
        def _():
            to(pa.at[rows(4 * f + i)], amid1.at[r], 1, {"resp": member}).start()

    @pl.when(is_mid)
    def _():
        amid1[r] = pa[rows(4 * f + z_hi), :]

    lane_at = lax.rem(lax.broadcasted_iota(jnp.int32, (T, 256), 1), T)
    visible = lax.broadcasted_iota(jnp.int32, (T, 256), 0) <= lane_at
    loads[4].wait()
    loads[5].wait()

    def own_head(h, carry):
        at = pl.multiple_of(h * HD, HD)
        keys = kv_own[0:128, pl.ds(at, HD)]
        values = kv_own[128:256, pl.ds(at, HD)]

        def heads(ref, g, count):
            return jnp.concatenate(
                [ref[:, pl.ds(pl.multiple_of(h * 1024 + (g + i) * HD, HD), HD)] for i in range(count)], axis=0
            )

        for g in range(0, 8, 2):
            probs, dscores = backward_tile(keys, values, heads(pq, g, 2), heads(pg, g, 2), visible, None, 0)
            probs_s[0, 0:128, g * HD:(g + 2) * HD] = probs
            dsc_s[0, 0:128, g * HD:(g + 2) * HD] = dscores
        dkv[0:128, pl.ds(at, HD)] = (mm(dsc_s[0, 0:128, :], heads(pq, 0, 8), NN) * FACTOR).astype(jnp.bfloat16)
        dkv[0:128, pl.ds(pl.multiple_of(256 + h * HD, HD), HD)] = mm(
            probs_s[0, 0:128, :], heads(pg, 0, 8), NN
        ).astype(jnp.bfloat16)
        return carry

    lax.fori_loop(0, 2, own_head, 0)

    loads[12].wait()
    ready(mid1.at[pl.ds(0, 15)], recv_sem.at[0])
    for k in RESP_ORDER:
        peer = lax.rem(r + k, N)
        mid2[peer] = mid1[pairing[0, peer]]
        to(mid2.at[peer], kv_pre.at[rows(r)], 2, {"resp": peer}).start()
    kv_pre[rows(r), :] = mid1[pairing[0, r]]

    @pl.when(is_mid)
    def _():
        ready(amid1.at[pl.ds(0, 15)], recv_sem.at[1])
        for k in RESP_ORDER:
            peer = lax.rem(r + k, N)
            amid2[peer] = amid1[pairing[0, peer]]
            to(amid2.at[peer], a_pre.at[rows(4 * f + z_hi)], 3, {"resp": peer}).start()
        a_pre[rows(4 * f + z_hi), :] = amid1[pairing[0, r]]

    own_proj[...] = mm(dkv[0:128, :], wide_up[...], NT)
    own_half[...] = own_proj[rows(1 - f, 64), :].astype(jnp.bfloat16)
    own_copy = to(own_half, own_twin, 4, twin)
    own_copy.start()
    for load in loads[6:12]:
        load.wait()
    lifted_slots = mm(aa[...], wide_up[...], NN)
    kv_slot[:, 0:256] = (ak[...].astype(jnp.float32) + lifted_slots[:, 0:256]).astype(jnp.bfloat16)
    kv_slot[:, 256:512] = (av[...].astype(jnp.float32) + lifted_slots[:, 256:512]).astype(jnp.bfloat16)
    outer_acc[...] = mm(pa[...], dkv[0:128, :], TN)

    ready(kv_pre.at[pl.ds(0, 240)], recv_sem.at[2])
    row_at = lax.rem(lax.broadcasted_iota(jnp.int32, (1, 256), 1), T)

    def slot_head(h, carry):
        at = pl.multiple_of(h * HD, HD)
        value_at = pl.multiple_of(256 + h * HD, HD)
        key_sum, value_sum = 0.0, 0.0
        for c in range(2):
            part = slice(c * T, (c + 1) * T)
            keys = jnp.concatenate([kv_pre[0:128, pl.ds(at, HD)], kv_slot[part, pl.ds(at, HD)]], axis=0)
            values = jnp.concatenate([kv_pre[128:256, pl.ds(at, HD)], kv_slot[part, pl.ds(value_at, HD)]], axis=0)
            live = row_at < lens[0, c]

            def heads(ref, g, count):
                return jnp.concatenate(
                    [ref[part, pl.ds(pl.multiple_of(h * 1024 + (g + i) * HD, HD), HD)] for i in range(count)], axis=0
                )

            for g in range(0, 8, 2):
                probs, dscores = backward_tile(keys, values, heads(aq, g, 2), heads(ag, g, 2), visible, live, T)
                probs_s[c, :, g * HD:(g + 2) * HD] = probs
                dsc_s[c, :, g * HD:(g + 2) * HD] = dscores
            key_grad = mm(dsc_s[c], heads(aq, 0, 8), NN) * FACTOR
            value_grad = mm(probs_s[c], heads(ag, 0, 8), NN)
            dkv[256 + c * T:256 + (c + 1) * T, pl.ds(at, HD)] = key_grad[T:].astype(jnp.bfloat16)
            dkv[256 + c * T:256 + (c + 1) * T, pl.ds(value_at, HD)] = value_grad[T:].astype(jnp.bfloat16)
            key_sum = key_sum + key_grad[:T]
            value_sum = value_sum + value_grad[:T]
        dkv[128:256, pl.ds(at, HD)] = key_sum.astype(jnp.bfloat16)
        dkv[128:256, pl.ds(value_at, HD)] = value_sum.astype(jnp.bfloat16)
        return carry

    @pl.when(is_mid)
    def _():
        ready(a_pre.at[pl.ds(0, 48)], recv_sem.at[3])

    @pl.when(jnp.logical_not(is_mid))
    def _():
        ready(a_pre.at[pl.ds(0, 64)], recv_sem.at[3])

    a_copy = to(a_pre.at[rows(f, 64)], a_pre.at[rows(f, 64)], 5, twin)
    a_copy.start()

    lax.fori_loop(0, 2, slot_head, 0)

    pre_part[...] = mm(dkv[128:256, :], wide_up[...], NT)
    pre_half[0] = pre_part[rows(1 - f, 64), :].astype(jnp.bfloat16)
    pre_copy = to(pre_half.at[0], pre_twin, 6, twin)
    pre_copy.start()

    ready(a_pre.at[pl.ds(0, 64)], recv_sem.at[5])
    outer = outer_acc[...] + mm(a_pre[...], dkv[128:256, :], TN) + mm(aa[...], dkv[256:512, :], TN)
    for b, (row, col) in enumerate([(0, 0), (0, 128), (64, 256), (64, 384)]):
        gr_send[4 * b:4 * b + 4] = outer[row:row + 64, col:col + 128].astype(jnp.bfloat16).reshape(4, 16, 128)
    for k in PLANE_ORDER:
        peer = (lax.rem(y + k // 4, 4)) * 4 + lax.rem(x + k % 4, 4)
        to(gr_send.at[peer], gr1.at[plane], 7, in_plane(peer)).start()
    gr1[plane] = gr_send[plane]

    ready(pre_twin, recv_sem.at[6])
    pre_half[1] = (pre_part[rows(f, 64), :] + pre_twin[...].astype(jnp.float32)).astype(jnp.bfloat16)
    for k in (2, 1, 3):
        peer_x = lax.rem(x + k, 4)
        to(pre_half.at[1, rows(peer_x)], pre_x.at[x], 8, {"resp": z_hi * 4 + peer_x}).start()
    pre_x[x] = pre_half[1, rows(x), :]

    an_send[...] = mm(dkv[256:512, :], wide_up[...], NT).astype(jnp.bfloat16)
    to_twin = to(an_send, an_recv, 9, twin)
    to_twin.start()

    ready(pre_x.at[pl.ds(0, 3)], recv_sem.at[8])
    for k in (2, 1, 3):
        to(pre_x, pre_z.at[z_hi], 10, {"resp": along_z(k)}).start()
    pre_z[z_hi] = pre_x[...]

    ready(gr1.at[pl.ds(0, 15)], recv_sem.at[7])
    part_sum = jnp.sum(gr1[...].astype(jnp.float32), axis=0).astype(jnp.bfloat16)
    gr2_send[...] = part_sum
    for k in RING_ORDER:
        to(gr2_send, gr2.at[ring], 11, in_ring(lax.rem(ring + k, N))).start()
    gr2[ring] = part_sum

    ready(an_recv, recv_sem.at[9])
    answer_out[0] = an_send[...].astype(jnp.float32) + an_recv[...].astype(jnp.float32)

    def responder(owner):
        held = jnp.int32(0)
        for d in range(N):
            held = jnp.where(pairing[0, d] == owner, d, held)
        return held

    sources = [responder(along_x(k)) for k in range(4)]
    ready(own_twin, recv_sem.at[4])
    ready(pre_z.at[pl.ds(0, 3)], recv_sem.at[10])
    for k in (2, 1, 3):
        pre_pick[k] = pre_z[sources[k] // 4, lax.rem(sources[k], 4)]
        to(pre_pick.at[k], pre_home.at[x], 12, {"resp": along_x(k)}).start()
    pre_home[x] = pre_z[sources[0] // 4, lax.rem(sources[0], 4)]

    ready(gr2.at[pl.ds(0, 15)], recv_sem.at[11])
    total = (jnp.sum(gr2[...].astype(jnp.float32), axis=0) * scale).astype(jnp.bfloat16)
    gr3_send[...] = total
    for k in PLANE_ORDER:
        peer = (lax.rem(y + k // 4, 4)) * 4 + lax.rem(x + k % 4, 4)
        to(gr3_send, gr3.at[plane], 13, in_plane(peer)).start()
    gr3[plane] = total

    ready(pre_home.at[pl.ds(0, 3)], recv_sem.at[12])
    done = (
        own_proj[rows(f, 64), :]
        + own_twin[...].astype(jnp.float32)
        + pre_home[...].reshape(64, 128).astype(jnp.float32)
    )
    done_half[...] = done
    done_copy = to(done_half, done_twin, 14, twin)
    done_copy.start()
    prompt_out[0, rows(f, 64), :] = done
    ready(done_twin, recv_sem.at[14])
    prompt_out[0, rows(1 - f, 64), :] = done_twin[...]

    ready(gr3.at[pl.ds(0, 15)], recv_sem.at[13])
    for b in range(4):
        up_out[b // 2, :, (b % 2) * 128:(b % 2) * 128 + 128] = (
            gr3[4 * b:4 * b + 4].reshape(64, 128).astype(jnp.float32)
        )

    ready(mid1.at[pl.ds(0, 15)], send_sem.at[0])
    ready(mid2.at[pl.ds(0, 15)], send_sem.at[2])
    own_copy.wait_send()
    a_copy.wait_send()
    pre_copy.wait_send()
    ready(gr_send.at[pl.ds(0, 15)], send_sem.at[7])
    ready(pre_x.at[pl.ds(0, 3)], send_sem.at[8])
    to_twin.wait_send()
    ready(pre_z.at[pl.ds(0, 3)], send_sem.at[10])
    ready(gr2.at[pl.ds(0, 15)], send_sem.at[11])
    ready(pre_pick.at[pl.ds(0, 3)], send_sem.at[12])
    ready(gr3.at[pl.ds(0, 15)], send_sem.at[13])
    done_copy.wait_send()

    @pl.when(is_mid)
    def _():
        ready(amid1.at[pl.ds(0, 3)], send_sem.at[1])
        ready(amid2.at[pl.ds(0, 15)], send_sem.at[3])

    @pl.when(jnp.logical_not(is_mid))
    def _():
        ready(amid1.at[pl.ds(0, 4)], send_sem.at[1])


def on_device(scale, *args):
    bf, f32 = jnp.bfloat16, jnp.float32
    hbm = pl.BlockSpec(memory_space=pltpu.HBM)
    vmem = pl.BlockSpec(memory_space=pltpu.VMEM)
    V = pltpu.VMEM
    return pl.pallas_call(
        functools.partial(kernel, scale),
        out_shape=(
            jax.ShapeDtypeStruct((1, 128, 128), f32),
            jax.ShapeDtypeStruct((1, 256, 128), f32),
            jax.ShapeDtypeStruct((2, 64, 256), f32),
        ),
        in_specs=[hbm] * 13,
        out_specs=(vmem, vmem, vmem),
        scratch_shapes=[
            V((128, 2048), bf), V((128, 256), bf), V((128, 256), bf), V((128, 128), bf), V((128, 2048), bf),
            V((256, 2048), bf), V((256, 256), bf), V((256, 256), bf), V((256, 128), bf), V((256, 2048), bf),
            V((2, 64, 256), bf), pltpu.SMEM((1, 2), jnp.int32), pltpu.SMEM((1, 16), jnp.int32),
            V((128, 512), bf), V((256, 256), bf), V((256, 512), bf), V((256, 256), bf),
            V((16, 16, 256), bf), V((16, 16, 256), bf), V((16, 16, 128), bf), V((16, 16, 128), bf), V((128, 128), bf),
            V((2, 256, 1024), bf), V((2, 256, 1024), bf), V((512, 512), bf), V((128, 128), f32), V((128, 512), f32),
            V((64, 128), bf), V((64, 128), bf), V((128, 128), f32), V((64, 128), bf), V((2, 64, 128), bf),
            V((4, 16, 128), bf), V((4, 4, 16, 128), bf), V((4, 16, 128), bf), V((4, 16, 128), bf),
            V((64, 128), f32), V((64, 128), f32),
            V((256, 128), bf), V((256, 128), bf),
            V((16, 16, 128), bf), V((16, 16, 128), bf), V((16, 128), bf), V((16, 16, 128), bf),
            V((16, 128), bf), V((16, 16, 128), bf),
            pltpu.SemaphoreType.DMA((13,)), pltpu.SemaphoreType.DMA((15,)), pltpu.SemaphoreType.DMA((15,)),
        ],
        compiler_params=pltpu.CompilerParams(
            collective_id=0, has_side_effects=True, vmem_limit_bytes=60 * 1024 * 1024
        ),
        name="adapter_backward",
    )(*args)


def solution(mesh):
    rows = ("prompt", "resp")
    wide = P(rows, None, "fsdp")
    whole = P(rows, None, None)
    scale = 1.0 / math.sqrt(mesh.shape["prompt"] * mesh.shape["resp"] * 2 * T)
    return jax.shard_map(
        functools.partial(on_device, scale),
        mesh=mesh,
        in_specs=(
            wide, wide, wide, whole, wide, wide, wide, wide, whole, wide,
            P(None, None, "fsdp"), P(rows, None), P("prompt", None),
        ),
        out_specs=(whole, whole, P(None, None, "fsdp")),
        check_vma=False,
    )
```

```python
import functools
import math

import jax
import jax.numpy as jnp
from jax import lax
from jax.experimental import pallas as pl
from jax.experimental.pallas import tpu as pltpu
from jax.sharding import PartitionSpec as P

MESH = pl.DeviceIdType.MESH
HD = 128
T = 128
N = 16
NT = (((1,), (1,)), ((), ()))
TN = (((0,), (0,)), ((), ()))
NN = (((1,), (0,)), ((), ()))
FACTOR = 1.0 / math.sqrt(HD)
EXP2_FACTOR = FACTOR * math.log2(math.e)
RESP_ORDER = (10, 9, 11, 8, 6, 14, 5, 7, 13, 15, 4, 12, 2, 1, 3)
PLANE_ORDER = (10, 9, 11, 6, 14, 8, 2, 5, 7, 13, 15, 4, 12, 1, 3)
RING_ORDER = (8, 7, 9, 6, 10, 5, 11, 4, 12, 3, 13, 2, 14, 1, 15)


def mm(a, b, dims):
    return lax.dot_general(a, b, dims, preferred_element_type=jnp.float32)


def ready(ref, sem):
    pltpu.make_async_copy(ref, ref, sem).wait()


def backward_tile(keys, values, queries, grads, visible, live, prefix):
    scores = mm(keys, queries, NT)
    dprobs = mm(values, grads, NT)
    own = jnp.where(visible, scores[prefix:], -1e30)
    highest = jnp.max(own, axis=0, keepdims=True)
    if prefix:
        highest = jnp.maximum(highest, jnp.max(scores[:prefix], axis=0, keepdims=True))
        scores = jnp.concatenate([scores[:prefix], own], axis=0)
    else:
        scores = own
    weights = jnp.exp2((scores - highest) * EXP2_FACTOR)
    inverse = 1.0 / jnp.sum(weights, axis=0, keepdims=True)
    if live is not None:
        inverse = jnp.where(live, inverse, 0.0)
    probs = weights * inverse
    delta = jnp.sum(probs * dprobs, axis=0, keepdims=True)
    dscores = probs * (dprobs - delta)
    return probs.astype(jnp.bfloat16), dscores.astype(jnp.bfloat16)


def joined_tile(keys, values, queries, grads, own_weights, own_dprobs, own_stats, live):
    scores = mm(keys, queries, NT)
    dprobs = mm(values, grads, NT)
    own_highest, own_sum, own_dot = own_stats[0:1], own_stats[1:2], own_stats[2:3]
    highest = jnp.maximum(own_highest, jnp.max(scores, axis=0, keepdims=True))
    weights = jnp.exp2((scores - highest) * EXP2_FACTOR)
    rescale = jnp.exp2((own_highest - highest) * EXP2_FACTOR)
    total = own_sum * rescale + jnp.sum(weights, axis=0, keepdims=True)
    inverse = jnp.where(live, 1.0 / total, 0.0)
    delta = (own_dot * rescale + jnp.sum(weights * dprobs, axis=0, keepdims=True)) * inverse
    probs = weights * inverse
    own_probs = own_weights * (rescale * inverse)
    return (
        probs.astype(jnp.bfloat16),
        (probs * (dprobs - delta)).astype(jnp.bfloat16),
        own_probs.astype(jnp.bfloat16),
        (own_probs * (own_dprobs - delta)).astype(jnp.bfloat16),
    )


def kernel(
    scale,
    pq_h, pk_h, pv_h, pa_h, pg_h, aq_h, ak_h, av_h, aa_h, ag_h, up_h, lens_h, pairing_h,
    prompt_out, answer_out, up_out,
    pq, pk, pv, pa, pg, aq, ak, av, aa, ag, up, lens, pairing,
    wide_up, kv_own, kv_slot, kv_pre, mid1, mid2, amid1, amid2, a_pre, a_cols, own_w, own_dp, own_st,
    probs_s, dsc_s, dkv, own_proj, outer_acc,
    own_half, own_twin, pre_part, pre_twin, pre_half, pre_x, pre_z, pre_pick, pre_home, done_half, done_twin,
    an_send, an_recv, gr_send, gr1, gr2_send, gr2, gr3_send, gr3,
    load_sem, send_sem, recv_sem,
):
    f = lax.axis_index("fsdp")
    p = lax.axis_index("prompt")
    r = lax.axis_index("resp")
    twin = {"fsdp": 1 - f}
    x, z_hi = lax.rem(r, 4), r // 4
    y, z_lo = p // 4, lax.rem(p, 4)
    is_mid = lax.rem(r, 4) == 2 * f
    plane = y * 4 + x
    ring = z_hi * 4 + z_lo

    def in_plane(at):
        return {"prompt": (at // 4) * 4 + z_lo, "resp": z_hi * 4 + lax.rem(at, 4)}

    def in_ring(at):
        return {"prompt": y * 4 + lax.rem(at, 4), "resp": (at // 4) * 4 + x}

    def along_x(k):
        return z_hi * 4 + lax.rem(x + k, 4)

    def along_z(k):
        return lax.rem(z_hi + k, 4) * 4 + x

    barrier = pltpu.get_barrier_semaphore()

    def greet(where):
        pl.semaphore_signal(barrier, inc=1, device_id=where, device_id_type=MESH)

    for k in RESP_ORDER:
        greet({"resp": lax.rem(r + k, N)})

    loads = [
        pltpu.make_async_copy(src.at[0] if lead else src, dst, load_sem.at[i])
        for i, (src, dst, lead) in enumerate([
            (up_h, up, False), (pa_h, pa, True), (pk_h, pk, True), (pv_h, pv, True),
            (pq_h, pq, True), (pg_h, pg, True), (aa_h, aa, True), (ak_h, ak, True),
            (av_h, av, True), (aq_h, aq, True), (ag_h, ag, True), (lens_h, lens, False), (pairing_h, pairing, False),
        ])
    ]
    for load in loads:
        load.start()

    greet(twin)
    for k in range(4, N):
        greet({"prompt": (lax.rem(y + k // 4, 4)) * 4 + z_lo, "resp": along_x(k % 4)})
    for k in range(4, N):
        greet({"prompt": y * 4 + lax.rem(z_lo + k // 4, 4), "resp": along_z(k % 4)})

    wide_up[...] = jnp.zeros_like(wide_up)
    for load in loads[:4]:
        load.wait()
    wide_up[0:64, 0:256] = up[0]
    wide_up[64:128, 256:512] = up[1]
    lifted = mm(pa[...], wide_up[...], NN)
    kv_own[0:128, :] = (pk[...].astype(jnp.float32) + lifted[:, 0:256]).astype(jnp.bfloat16)
    kv_own[128:256, :] = (pv[...].astype(jnp.float32) + lifted[:, 256:512]).astype(jnp.bfloat16)

    pl.semaphore_wait(barrier, 40)

    def to(src, dst, lane, where):
        return pltpu.make_async_remote_copy(
            src_ref=src, dst_ref=dst, send_sem=send_sem.at[lane], recv_sem=recv_sem.at[lane],
            device_id=where, device_id_type=MESH,
        )

    def rows(index, size=16):
        return pl.ds(pl.multiple_of(index * size, size), size)

    for k in RESP_ORDER:
        peer = lax.rem(r + k, N)
        to(kv_own.at[rows(peer)], mid1.at[r], 0, {"resp": peer}).start()
    mid1[r] = kv_own[rows(r), :]
    for i in range(4):
        member = 4 * i + 2 * f

        @pl.when(member != r)
        def _():
            to(pa.at[rows(4 * f + i)], amid1.at[r], 1, {"resp": member}).start()

    @pl.when(is_mid)
    def _():
        amid1[r] = pa[rows(4 * f + z_hi), :]

    lane_at = lax.rem(lax.broadcasted_iota(jnp.int32, (T, 256), 1), T)
    visible = lax.broadcasted_iota(jnp.int32, (T, 256), 0) <= lane_at
    loads[4].wait()
    loads[5].wait()

    def own_head(h, carry):
        at = pl.multiple_of(h * HD, HD)
        keys = kv_own[0:128, pl.ds(at, HD)]
        values = kv_own[128:256, pl.ds(at, HD)]

        def heads(ref, g, count):
            return jnp.concatenate(
                [ref[:, pl.ds(pl.multiple_of(h * 1024 + (g + i) * HD, HD), HD)] for i in range(count)], axis=0
            )

        for g in range(0, 8, 2):
            probs, dscores = backward_tile(keys, values, heads(pq, g, 2), heads(pg, g, 2), visible, None, 0)
            probs_s[0, 0:128, g * HD:(g + 2) * HD] = probs
            dsc_s[0, 0:128, g * HD:(g + 2) * HD] = dscores
        dkv[0:128, pl.ds(at, HD)] = (mm(dsc_s[0, 0:128, :], heads(pq, 0, 8), NN) * FACTOR).astype(jnp.bfloat16)
        dkv[0:128, pl.ds(pl.multiple_of(256 + h * HD, HD), HD)] = mm(
            probs_s[0, 0:128, :], heads(pg, 0, 8), NN
        ).astype(jnp.bfloat16)
        return carry

    lax.fori_loop(0, 2, own_head, 0)

    loads[12].wait()
    ready(mid1.at[pl.ds(0, 15)], recv_sem.at[0])
    for k in RESP_ORDER:
        peer = lax.rem(r + k, N)
        mid2[peer] = mid1[pairing[0, peer]]
        to(mid2.at[peer], kv_pre.at[rows(r)], 2, {"resp": peer}).start()
    kv_pre[rows(r), :] = mid1[pairing[0, r]]

    @pl.when(is_mid)
    def _():
        ready(amid1.at[pl.ds(0, 15)], recv_sem.at[1])
        for k in RESP_ORDER:
            peer = lax.rem(r + k, N)
            amid2[peer] = amid1[pairing[0, peer]]
            to(amid2.at[peer], a_pre.at[rows(4 * f + z_hi)], 3, {"resp": peer}).start()
        a_pre[rows(4 * f + z_hi), :] = amid1[pairing[0, r]]

    own_proj[...] = mm(dkv[0:128, :], wide_up[...], NT)
    own_half[...] = own_proj[rows(1 - f, 64), :].astype(jnp.bfloat16)
    own_copy = to(own_half, own_twin, 4, twin)
    own_copy.start()
    for load in loads[6:12]:
        load.wait()
    lifted_slots = mm(aa[...], wide_up[...], NN)
    kv_slot[:, 0:256] = (ak[...].astype(jnp.float32) + lifted_slots[:, 0:256]).astype(jnp.bfloat16)
    kv_slot[:, 256:512] = (av[...].astype(jnp.float32) + lifted_slots[:, 256:512]).astype(jnp.bfloat16)
    outer_acc[...] = mm(pa[...], dkv[0:128, :], TN)
    a_cols[:, 128:256] = jnp.transpose(aa[0:128, :])
    a_cols[:, 256:384] = jnp.transpose(aa[128:256, :])

    row_at = lax.rem(lax.broadcasted_iota(jnp.int32, (1, 256), 1), T)

    def heads(ref, c, h, g, count):
        return jnp.concatenate(
            [ref[c * T:(c + 1) * T, (8 * h + g + i) * HD:(8 * h + g + i + 1) * HD] for i in range(count)], axis=0
        )

    for h in range(2):
        for c in range(2):
            keys = kv_slot[c * T:(c + 1) * T, h * HD:(h + 1) * HD]
            values = kv_slot[c * T:(c + 1) * T, 256 + h * HD:256 + (h + 1) * HD]
            for g in range(0, 8, 2):
                cols = slice(g * HD, (g + 2) * HD)
                scores = jnp.where(visible, mm(keys, heads(aq, c, h, g, 2), NT), -1e30)
                dprobs = mm(values, heads(ag, c, h, g, 2), NT)
                highest = jnp.max(scores, axis=0, keepdims=True)
                weights = jnp.exp2((scores - highest) * EXP2_FACTOR)
                own_w[2 * h + c, :, cols] = weights
                own_dp[2 * h + c, :, cols] = dprobs
                own_st[2 * h + c, 0:1, cols] = highest
                own_st[2 * h + c, 1:2, cols] = jnp.sum(weights, axis=0, keepdims=True)
                own_st[2 * h + c, 2:3, cols] = jnp.sum(weights * dprobs, axis=0, keepdims=True)

    def slot_head(h):
        key_cols = slice(h * HD, (h + 1) * HD)
        value_cols = slice(256 + h * HD, 256 + (h + 1) * HD)
        keys, values = kv_pre[0:128, key_cols], kv_pre[128:256, key_cols]
        key_sum, value_sum = 0.0, 0.0
        for c in range(2):
            live = row_at < lens[0, c]
            for g in range(0, 8, 2):
                cols = slice(g * HD, (g + 2) * HD)
                probs, dscores, own_probs, own_dscores = joined_tile(
                    keys, values, heads(aq, c, h, g, 2), heads(ag, c, h, g, 2),
                    own_w[2 * h + c, :, cols], own_dp[2 * h + c, :, cols], own_st[2 * h + c, :, cols], live,
                )
                probs_s[c, 0:128, cols] = probs
                probs_s[c, 128:256, cols] = own_probs
                dsc_s[c, 0:128, cols] = dscores
                dsc_s[c, 128:256, cols] = own_dscores
            key_grad = mm(dsc_s[c], heads(aq, c, h, 0, 8), NN) * FACTOR
            value_grad = mm(probs_s[c], heads(ag, c, h, 0, 8), NN)
            dkv[256 + c * T:256 + (c + 1) * T, key_cols] = key_grad[T:].astype(jnp.bfloat16)
            dkv[256 + c * T:256 + (c + 1) * T, value_cols] = value_grad[T:].astype(jnp.bfloat16)
            key_sum = key_sum + key_grad[:T]
            value_sum = value_sum + value_grad[:T]
        dkv[128:256, key_cols] = key_sum.astype(jnp.bfloat16)
        dkv[128:256, value_cols] = value_sum.astype(jnp.bfloat16)

    ready(kv_pre.at[pl.ds(0, 240)], recv_sem.at[2])
    slot_head(0)

    @pl.when(is_mid)
    def _():
        ready(a_pre.at[pl.ds(0, 48)], recv_sem.at[3])

    @pl.when(jnp.logical_not(is_mid))
    def _():
        ready(a_pre.at[pl.ds(0, 64)], recv_sem.at[3])

    a_copy = to(a_pre.at[rows(f, 64)], a_pre.at[rows(f, 64)], 5, twin)
    a_copy.start()
    slot_head(1)

    ready(a_pre.at[pl.ds(0, 64)], recv_sem.at[5])
    a_cols[:, 0:128] = jnp.transpose(a_pre[...])
    for b, (row, col) in enumerate([(0, 0), (0, 128), (64, 256), (64, 384)]):
        block = outer_acc[row:row + 64, col:col + 128] + mm(
            a_cols[row:row + 64, :], dkv[128:512, col:col + 128], NN
        )
        gr_send[4 * b:4 * b + 4] = block.astype(jnp.bfloat16).reshape(4, 16, 128)
    for k in PLANE_ORDER:
        peer = (lax.rem(y + k // 4, 4)) * 4 + lax.rem(x + k % 4, 4)
        to(gr_send.at[peer], gr1.at[plane], 7, in_plane(peer)).start()
    gr1[plane] = gr_send[plane]

    pre_part[...] = mm(dkv[128:256, :], wide_up[...], NT)
    pre_half[0] = pre_part[rows(1 - f, 64), :].astype(jnp.bfloat16)
    pre_copy = to(pre_half.at[0], pre_twin, 6, twin)
    pre_copy.start()

    ready(pre_twin, recv_sem.at[6])
    pre_half[1] = (pre_part[rows(f, 64), :] + pre_twin[...].astype(jnp.float32)).astype(jnp.bfloat16)
    for k in (2, 1, 3):
        peer_x = lax.rem(x + k, 4)
        to(pre_half.at[1, rows(peer_x)], pre_x.at[x], 8, {"resp": z_hi * 4 + peer_x}).start()
    pre_x[x] = pre_half[1, rows(x), :]

    an_send[...] = mm(dkv[256:512, :], wide_up[...], NT).astype(jnp.bfloat16)
    to_twin = to(an_send, an_recv, 9, twin)
    to_twin.start()

    ready(pre_x.at[pl.ds(0, 3)], recv_sem.at[8])
    for k in (2, 1, 3):
        to(pre_x, pre_z.at[z_hi], 10, {"resp": along_z(k)}).start()
    pre_z[z_hi] = pre_x[...]

    ready(gr1.at[pl.ds(0, 15)], recv_sem.at[7])
    part_sum = jnp.sum(gr1[...].astype(jnp.float32), axis=0).astype(jnp.bfloat16)
    gr2_send[...] = part_sum
    for k in RING_ORDER:
        to(gr2_send, gr2.at[ring], 11, in_ring(lax.rem(ring + k, N))).start()
    gr2[ring] = part_sum

    ready(an_recv, recv_sem.at[9])
    answer_out[0] = an_send[...].astype(jnp.float32) + an_recv[...].astype(jnp.float32)

    def responder(owner):
        held = jnp.int32(0)
        for d in range(N):
            held = jnp.where(pairing[0, d] == owner, d, held)
        return held

    sources = [responder(along_x(k)) for k in range(4)]
    ready(own_twin, recv_sem.at[4])
    ready(pre_z.at[pl.ds(0, 3)], recv_sem.at[10])
    for k in (2, 1, 3):
        pre_pick[k] = pre_z[sources[k] // 4, lax.rem(sources[k], 4)]
        to(pre_pick.at[k], pre_home.at[x], 12, {"resp": along_x(k)}).start()
    pre_home[x] = pre_z[sources[0] // 4, lax.rem(sources[0], 4)]

    ready(gr2.at[pl.ds(0, 15)], recv_sem.at[11])
    total = (jnp.sum(gr2[...].astype(jnp.float32), axis=0) * scale).astype(jnp.bfloat16)
    gr3_send[...] = total
    for k in PLANE_ORDER:
        peer = (lax.rem(y + k // 4, 4)) * 4 + lax.rem(x + k % 4, 4)
        to(gr3_send, gr3.at[plane], 13, in_plane(peer)).start()
    gr3[plane] = total

    ready(pre_home.at[pl.ds(0, 3)], recv_sem.at[12])
    done = (
        own_proj[rows(f, 64), :]
        + own_twin[...].astype(jnp.float32)
        + pre_home[...].reshape(64, 128).astype(jnp.float32)
    )
    done_half[...] = done
    done_copy = to(done_half, done_twin, 14, twin)
    done_copy.start()
    prompt_out[0, rows(f, 64), :] = done
    ready(done_twin, recv_sem.at[14])
    prompt_out[0, rows(1 - f, 64), :] = done_twin[...]

    ready(gr3.at[pl.ds(0, 15)], recv_sem.at[13])
    for b in range(4):
        up_out[b // 2, :, (b % 2) * 128:(b % 2) * 128 + 128] = (
            gr3[4 * b:4 * b + 4].reshape(64, 128).astype(jnp.float32)
        )

    ready(mid1.at[pl.ds(0, 15)], send_sem.at[0])
    ready(mid2.at[pl.ds(0, 15)], send_sem.at[2])
    own_copy.wait_send()
    a_copy.wait_send()
    pre_copy.wait_send()
    ready(gr_send.at[pl.ds(0, 15)], send_sem.at[7])
    ready(pre_x.at[pl.ds(0, 3)], send_sem.at[8])
    to_twin.wait_send()
    ready(pre_z.at[pl.ds(0, 3)], send_sem.at[10])
    ready(gr2.at[pl.ds(0, 15)], send_sem.at[11])
    ready(pre_pick.at[pl.ds(0, 3)], send_sem.at[12])
    ready(gr3.at[pl.ds(0, 15)], send_sem.at[13])
    done_copy.wait_send()

    @pl.when(is_mid)
    def _():
        ready(amid1.at[pl.ds(0, 3)], send_sem.at[1])
        ready(amid2.at[pl.ds(0, 15)], send_sem.at[3])

    @pl.when(jnp.logical_not(is_mid))
    def _():
        ready(amid1.at[pl.ds(0, 4)], send_sem.at[1])


def store(a, b, c, a_out, b_out, c_out, sem):
    copies = [pltpu.make_async_copy(*pair, sem.at[i]) for i, pair in enumerate([(a, a_out), (b, b_out), (c, c_out)])]
    for copy in copies:
        copy.start()
    for copy in copies:
        copy.wait()


def on_device(scale, *args):
    bf, f32 = jnp.bfloat16, jnp.float32
    hbm = pl.BlockSpec(memory_space=pltpu.HBM)
    vmem = pl.BlockSpec(memory_space=pltpu.VMEM)
    V = pltpu.VMEM
    args = [pltpu.with_memory_space_constraint(a, pltpu.HBM) for a in args]
    held = pl.pallas_call(
        functools.partial(kernel, scale),
        out_shape=(
            jax.ShapeDtypeStruct((1, 128, 128), f32),
            jax.ShapeDtypeStruct((1, 256, 128), f32),
            jax.ShapeDtypeStruct((2, 64, 256), f32),
        ),
        in_specs=[hbm] * 13,
        out_specs=(vmem, vmem, vmem),
        scratch_shapes=[
            V((128, 2048), bf), V((128, 256), bf), V((128, 256), bf), V((128, 128), bf), V((128, 2048), bf),
            V((256, 2048), bf), V((256, 256), bf), V((256, 256), bf), V((256, 128), bf), V((256, 2048), bf),
            V((2, 64, 256), bf), pltpu.SMEM((1, 2), jnp.int32), pltpu.SMEM((1, 16), jnp.int32),
            V((128, 512), bf), V((256, 256), bf), V((256, 512), bf), V((256, 256), bf),
            V((16, 16, 256), bf), V((16, 16, 256), bf), V((16, 16, 128), bf), V((16, 16, 128), bf), V((128, 128), bf),
            V((128, 384), bf), V((4, 128, 1024), f32), V((4, 128, 1024), f32), V((4, 8, 1024), f32),
            V((2, 256, 1024), bf), V((2, 256, 1024), bf), V((512, 512), bf), V((128, 128), f32), V((128, 512), f32),
            V((64, 128), bf), V((64, 128), bf), V((128, 128), f32), V((64, 128), bf), V((2, 64, 128), bf),
            V((4, 16, 128), bf), V((4, 4, 16, 128), bf), V((4, 16, 128), bf), V((4, 16, 128), bf),
            V((64, 128), f32), V((64, 128), f32),
            V((256, 128), bf), V((256, 128), bf),
            V((16, 16, 128), bf), V((16, 16, 128), bf), V((16, 128), bf), V((16, 16, 128), bf),
            V((16, 128), bf), V((16, 16, 128), bf),
            pltpu.SemaphoreType.DMA((13,)), pltpu.SemaphoreType.DMA((15,)), pltpu.SemaphoreType.DMA((15,)),
        ],
        compiler_params=pltpu.CompilerParams(
            collective_id=0, has_side_effects=True, vmem_limit_bytes=48 * 1024 * 1024
        ),
        name="adapter_backward",
    )(*args)
    return pl.pallas_call(
        store,
        out_shape=tuple(jax.ShapeDtypeStruct(h.shape, h.dtype) for h in held),
        in_specs=[pl.BlockSpec(memory_space=pl.ANY)] * 3,
        out_specs=(pl.BlockSpec(memory_space=pl.ANY),) * 3,
        scratch_shapes=[pltpu.SemaphoreType.DMA((3,))],
        compiler_params=pltpu.CompilerParams(vmem_limit_bytes=65136 * 1024),
        name="store",
    )(*[pltpu.with_memory_space_constraint(h, pltpu.VMEM) for h in held])


def solution(mesh):
    rows = ("prompt", "resp")
    wide = P(rows, None, "fsdp")
    whole = P(rows, None, None)
    scale = 1.0 / math.sqrt(mesh.shape["prompt"] * mesh.shape["resp"] * 2 * T)
    return jax.shard_map(
        functools.partial(on_device, scale),
        mesh=mesh,
        in_specs=(
            wide, wide, wide, whole, wide, wide, wide, wide, whole, wide,
            P(None, None, "fsdp"), P(rows, None), P("prompt", None),
        ),
        out_specs=(whole, whole, P(None, None, "fsdp")),
        check_vma=False,
    )
```

```python
import functools
import math

import jax
import jax.numpy as jnp
from jax import lax
from jax.experimental import pallas as pl
from jax.experimental.pallas import tpu as pltpu
from jax.sharding import PartitionSpec as P

MESH = pl.DeviceIdType.MESH
HD = 128
T = 128
N = 16
NT = (((1,), (1,)), ((), ()))
TN = (((0,), (0,)), ((), ()))
NN = (((1,), (0,)), ((), ()))
FACTOR = 1.0 / math.sqrt(HD)
EXP2_FACTOR = FACTOR * math.log2(math.e)
SHIFTS = (0, 1, 3)
NEAR_ORDER = ((1, 2), (2, 2), (1, 1), (2, 1), (1, 3), (2, 3), (1, 0), (2, 0), (0, 2), (0, 1), (0, 3))
RESP_ORDER = (10, 9, 11, 8, 6, 14, 5, 7, 13, 15, 4, 12, 2, 1, 3)
PLANE_ORDER = (10, 9, 11, 6, 14, 8, 2, 5, 7, 13, 15, 4, 12, 1, 3)
RING_ORDER = (8, 7, 9, 6, 10, 5, 11, 4, 12, 3, 13, 2, 14, 1, 15)


def mm(a, b, dims):
    return lax.dot_general(a, b, dims, preferred_element_type=jnp.float32)


def ready(ref, sem):
    pltpu.make_async_copy(ref, ref, sem).wait()


def backward_tile(keys, values, queries, grads, visible, live, prefix):
    scores = mm(keys, queries, NT)
    dprobs = mm(values, grads, NT)
    own = jnp.where(visible, scores[prefix:], -1e30)
    highest = jnp.max(own, axis=0, keepdims=True)
    if prefix:
        highest = jnp.maximum(highest, jnp.max(scores[:prefix], axis=0, keepdims=True))
        scores = jnp.concatenate([scores[:prefix], own], axis=0)
    else:
        scores = own
    weights = jnp.exp2((scores - highest) * EXP2_FACTOR)
    inverse = 1.0 / jnp.sum(weights, axis=0, keepdims=True)
    if live is not None:
        inverse = jnp.where(live, inverse, 0.0)
    probs = weights * inverse
    delta = jnp.sum(probs * dprobs, axis=0, keepdims=True)
    dscores = probs * (dprobs - delta)
    return probs.astype(jnp.bfloat16), dscores.astype(jnp.bfloat16)


def joined_tile(keys, values, queries, grads, own_weights, own_dprobs, own_stats, live):
    scores = mm(keys, queries, NT)
    dprobs = mm(values, grads, NT)
    own_highest, own_sum, own_dot = own_stats[0:1], own_stats[1:2], own_stats[2:3]
    highest = jnp.maximum(own_highest, jnp.max(scores, axis=0, keepdims=True))
    weights = jnp.exp2((scores - highest) * EXP2_FACTOR)
    rescale = jnp.exp2((own_highest - highest) * EXP2_FACTOR)
    total = own_sum * rescale + jnp.sum(weights, axis=0, keepdims=True)
    inverse = jnp.where(live, 1.0 / total, 0.0)
    delta = (own_dot * rescale + jnp.sum(weights * dprobs, axis=0, keepdims=True)) * inverse
    probs = weights * inverse
    own_probs = own_weights * (rescale * inverse)
    return (
        probs.astype(jnp.bfloat16),
        (probs * (dprobs - delta)).astype(jnp.bfloat16),
        own_probs.astype(jnp.bfloat16),
        (own_probs * (own_dprobs - delta)).astype(jnp.bfloat16),
    )


def kernel(
    scale,
    pq_h, pk_h, pv_h, pa_h, pg_h, aq_h, ak_h, av_h, aa_h, ag_h, up_h, lens_h, pairing_h,
    prompt_out, answer_out, up_out,
    pq, pk, pv, pa, pg, aq, ak, av, aa, ag, up, lens, pairing,
    wide_up, pack, kv_slot, pre, mid1, mid2, got, a_pre, a_cols, own_w, own_dp, own_st,
    probs_s, dsc_s, dkv, own_proj, outer_acc,
    own_half, own_twin, pre_part, pre_twin, pre_half, pre_x, pre_z, pre_pick, pre_home, done_half, done_twin,
    an_send, an_recv, gr_send, gr1, gr2_send, gr2, gr3_send, gr3,
    load_sem, send_sem, recv_sem,
):
    f = lax.axis_index("fsdp")
    p = lax.axis_index("prompt")
    r = lax.axis_index("resp")
    twin = {"fsdp": 1 - f}
    x, z_hi = lax.rem(r, 4), r // 4
    y, z_lo = p // 4, lax.rem(p, 4)
    plane = y * 4 + x
    ring = z_hi * 4 + z_lo

    def in_plane(at):
        return {"prompt": (at // 4) * 4 + z_lo, "resp": z_hi * 4 + lax.rem(at, 4)}

    def in_ring(at):
        return {"prompt": y * 4 + lax.rem(at, 4), "resp": (at // 4) * 4 + x}

    def along_x(k):
        return z_hi * 4 + lax.rem(x + k, 4)

    def along_z(k):
        return lax.rem(z_hi + k, 4) * 4 + x

    barrier = pltpu.get_barrier_semaphore()

    def greet(where):
        pl.semaphore_signal(barrier, inc=1, device_id=where, device_id_type=MESH)

    for shift, k in NEAR_ORDER:
        greet({"resp": lax.rem(z_hi + SHIFTS[shift], 4) * 4 + lax.rem(x + k, 4)})

    loads = [
        pltpu.make_async_copy(src.at[0] if lead else src, dst, load_sem.at[i])
        for i, (src, dst, lead) in enumerate([
            (up_h, up, False), (pa_h, pa, True), (pk_h, pk, True), (pv_h, pv, True),
            (pq_h, pq, True), (pg_h, pg, True), (aa_h, aa, True), (ak_h, ak, True),
            (av_h, av, True), (aq_h, aq, True), (ag_h, ag, True), (lens_h, lens, False), (pairing_h, pairing, False),
        ])
    ]
    for load in loads:
        load.start()

    greet(twin)
    for k in range(4, N):
        greet({"prompt": (lax.rem(y + k // 4, 4)) * 4 + z_lo, "resp": along_x(k % 4)})
    for k in range(1, 4):
        greet({"prompt": y * 4 + lax.rem(z_lo + k, 4)})

    wide_up[...] = jnp.zeros_like(wide_up)
    for load in loads[:4]:
        load.wait()
    wide_up[0:64, 0:256] = up[0]
    wide_up[64:128, 256:512] = up[1]
    lifted = mm(pa[...], wide_up[...], NN)
    for i, base in enumerate((pk, pv)):
        full = (base[...].astype(jnp.float32) + lifted[:, 256 * i:256 * i + 256]).astype(jnp.bfloat16)
        for h in range(2):
            pack[16 * i + 8 * h:16 * i + 8 * h + 8] = full[:, h * HD:(h + 1) * HD].reshape(8, 16, HD)
    pack[32:36] = pa[pl.ds(pl.multiple_of(f * 64, 64), 64), :].reshape(4, 16, HD)

    pl.semaphore_wait(barrier, 27)

    def to(src, dst, lane, where):
        return pltpu.make_async_remote_copy(
            src_ref=src, dst_ref=dst, send_sem=send_sem.at[lane], recv_sem=recv_sem.at[lane],
            device_id=where, device_id_type=MESH,
        )

    def rows(index, size=16):
        return pl.ds(pl.multiple_of(index * size, size), size)

    for shift, k in NEAR_ORDER:
        peer_x = lax.rem(x + k, 4)
        peer = lax.rem(z_hi + SHIFTS[shift], 4) * 4 + peer_x
        to(pack.at[pl.ds(3 * (4 * shift + peer_x), 3)], mid1.at[r], 0, {"resp": peer}).start()
    mid1[r] = pack[pl.ds(3 * x, 3)]
    for k in range(4):
        mid1[lax.rem(z_hi + 2, 4) * 4 + k] = jnp.zeros((3, 16, HD), jnp.bfloat16)

    lane_at = lax.rem(lax.broadcasted_iota(jnp.int32, (T, 256), 1), T)
    visible = lax.broadcasted_iota(jnp.int32, (T, 256), 0) <= lane_at
    loads[4].wait()
    loads[5].wait()

    def own_head(h, carry):
        at = pl.multiple_of(h * HD, HD)
        keys = pack[pl.ds(8 * h, 8)].reshape(T, HD)
        values = pack[pl.ds(16 + 8 * h, 8)].reshape(T, HD)

        def heads(ref, g, count):
            return jnp.concatenate(
                [ref[:, pl.ds(pl.multiple_of(h * 1024 + (g + i) * HD, HD), HD)] for i in range(count)], axis=0
            )

        for g in range(0, 8, 2):
            probs, dscores = backward_tile(keys, values, heads(pq, g, 2), heads(pg, g, 2), visible, None, 0)
            probs_s[0, 0:128, g * HD:(g + 2) * HD] = probs
            dsc_s[0, 0:128, g * HD:(g + 2) * HD] = dscores
        dkv[0:128, pl.ds(at, HD)] = (mm(dsc_s[0, 0:128, :], heads(pq, 0, 8), NN) * FACTOR).astype(jnp.bfloat16)
        dkv[0:128, pl.ds(pl.multiple_of(256 + h * HD, HD), HD)] = mm(
            probs_s[0, 0:128, :], heads(pg, 0, 8), NN
        ).astype(jnp.bfloat16)
        return carry

    lax.fori_loop(0, 2, own_head, 0)

    loads[12].wait()
    ready(mid1.at[pl.ds(0, 11)], recv_sem.at[0])

    def held_of(member):
        owner = pairing[0, member]
        return jnp.where(lax.rem(owner // 4 + 6 - z_hi, 4) == 0, r, owner)

    for k in RESP_ORDER:
        peer = lax.rem(r + k, N)
        mid2[peer] = mid1[held_of(peer)]
        to(mid2.at[peer], got.at[r], 2, {"resp": peer}).start()
    got[r] = mid1[held_of(r)]

    own_proj[...] = mm(dkv[0:128, :], wide_up[...], NT)
    own_half[...] = own_proj[rows(1 - f, 64), :].astype(jnp.bfloat16)
    own_copy = to(own_half, own_twin, 4, twin)
    own_copy.start()
    for load in loads[6:12]:
        load.wait()
    lifted_slots = mm(aa[...], wide_up[...], NN)
    kv_slot[:, 0:256] = (ak[...].astype(jnp.float32) + lifted_slots[:, 0:256]).astype(jnp.bfloat16)
    kv_slot[:, 256:512] = (av[...].astype(jnp.float32) + lifted_slots[:, 256:512]).astype(jnp.bfloat16)
    outer_acc[...] = mm(pa[...], dkv[0:128, :], TN)
    a_cols[:, 128:256] = jnp.transpose(aa[0:128, :])
    a_cols[:, 256:384] = jnp.transpose(aa[128:256, :])

    row_at = lax.rem(lax.broadcasted_iota(jnp.int32, (1, 256), 1), T)

    def heads(ref, c, h, g, count):
        return jnp.concatenate(
            [ref[c * T:(c + 1) * T, (8 * h + g + i) * HD:(8 * h + g + i + 1) * HD] for i in range(count)], axis=0
        )

    for h in range(2):
        for c in range(2):
            keys = kv_slot[c * T:(c + 1) * T, h * HD:(h + 1) * HD]
            values = kv_slot[c * T:(c + 1) * T, 256 + h * HD:256 + (h + 1) * HD]
            for g in range(0, 8, 2):
                cols = slice(g * HD, (g + 2) * HD)
                scores = jnp.where(visible, mm(keys, heads(aq, c, h, g, 2), NT), -1e30)
                dprobs = mm(values, heads(ag, c, h, g, 2), NT)
                highest = jnp.max(scores, axis=0, keepdims=True)
                weights = jnp.exp2((scores - highest) * EXP2_FACTOR)
                own_w[2 * h + c, :, cols] = weights
                own_dp[2 * h + c, :, cols] = dprobs
                own_st[2 * h + c, 0:1, cols] = highest
                own_st[2 * h + c, 1:2, cols] = jnp.sum(weights, axis=0, keepdims=True)
                own_st[2 * h + c, 2:3, cols] = jnp.sum(weights * dprobs, axis=0, keepdims=True)

    def slot_head(h):
        key_cols = slice(h * HD, (h + 1) * HD)
        value_cols = slice(256 + h * HD, 256 + (h + 1) * HD)
        keys = pre[8 * h:8 * h + 8].reshape(T, HD)
        values = pre[16 + 8 * h:24 + 8 * h].reshape(T, HD)
        key_sum, value_sum = 0.0, 0.0
        for c in range(2):
            live = row_at < lens[0, c]
            for g in range(0, 8, 2):
                cols = slice(g * HD, (g + 2) * HD)
                probs, dscores, own_probs, own_dscores = joined_tile(
                    keys, values, heads(aq, c, h, g, 2), heads(ag, c, h, g, 2),
                    own_w[2 * h + c, :, cols], own_dp[2 * h + c, :, cols], own_st[2 * h + c, :, cols], live,
                )
                probs_s[c, 0:128, cols] = probs
                probs_s[c, 128:256, cols] = own_probs
                dsc_s[c, 0:128, cols] = dscores
                dsc_s[c, 128:256, cols] = own_dscores
            key_grad = mm(dsc_s[c], heads(aq, c, h, 0, 8), NN) * FACTOR
            value_grad = mm(probs_s[c], heads(ag, c, h, 0, 8), NN)
            dkv[256 + c * T:256 + (c + 1) * T, key_cols] = key_grad[T:].astype(jnp.bfloat16)
            dkv[256 + c * T:256 + (c + 1) * T, value_cols] = value_grad[T:].astype(jnp.bfloat16)
            key_sum = key_sum + key_grad[:T]
            value_sum = value_sum + value_grad[:T]
        dkv[128:256, key_cols] = key_sum.astype(jnp.bfloat16)
        dkv[128:256, value_cols] = value_sum.astype(jnp.bfloat16)

    ready(got.at[pl.ds(0, 15)], recv_sem.at[2])
    from_plane = pairing[0, r] // 4
    for shift in range(3):
        for k in range(4):
            at = 3 * (4 * shift + k)
            pre[at:at + 3] = got[lax.rem(from_plane + SHIFTS[shift], 4) * 4 + k]

    a_pre[rows(f, 64), :] = pre[32:36].reshape(64, HD)
    a_copy = to(a_pre.at[rows(f, 64)], a_pre.at[rows(f, 64)], 5, twin)
    a_copy.start()
    slot_head(0)
    slot_head(1)

    ready(a_pre.at[pl.ds(0, 64)], recv_sem.at[5])
    a_cols[:, 0:128] = jnp.transpose(a_pre[...])
    for b, (row, col) in enumerate([(0, 0), (0, 128), (64, 256), (64, 384)]):
        block = outer_acc[row:row + 64, col:col + 128] + mm(
            a_cols[row:row + 64, :], dkv[128:512, col:col + 128], NN
        )
        gr_send[4 * b:4 * b + 4] = block.astype(jnp.bfloat16).reshape(4, 16, 128)
    for k in PLANE_ORDER:
        peer = (lax.rem(y + k // 4, 4)) * 4 + lax.rem(x + k % 4, 4)
        to(gr_send.at[peer], gr1.at[plane], 7, in_plane(peer)).start()
    gr1[plane] = gr_send[plane]

    pre_part[...] = mm(dkv[128:256, :], wide_up[...], NT)
    pre_half[0] = pre_part[rows(1 - f, 64), :].astype(jnp.bfloat16)
    pre_copy = to(pre_half.at[0], pre_twin, 6, twin)
    pre_copy.start()

    ready(pre_twin, recv_sem.at[6])
    pre_half[1] = (pre_part[rows(f, 64), :] + pre_twin[...].astype(jnp.float32)).astype(jnp.bfloat16)
    for k in (2, 1, 3):
        peer_x = lax.rem(x + k, 4)
        to(pre_half.at[1, rows(peer_x)], pre_x.at[x], 8, {"resp": z_hi * 4 + peer_x}).start()
    pre_x[x] = pre_half[1, rows(x), :]

    an_send[...] = mm(dkv[256:512, :], wide_up[...], NT).astype(jnp.bfloat16)
    to_twin = to(an_send, an_recv, 9, twin)
    to_twin.start()

    ready(pre_x.at[pl.ds(0, 3)], recv_sem.at[8])
    for k in (2, 1, 3):
        to(pre_x, pre_z.at[z_hi], 10, {"resp": along_z(k)}).start()
    pre_z[z_hi] = pre_x[...]

    ready(gr1.at[pl.ds(0, 15)], recv_sem.at[7])
    part_sum = jnp.sum(gr1[...].astype(jnp.float32), axis=0).astype(jnp.bfloat16)
    gr2_send[...] = part_sum
    for k in RING_ORDER:
        to(gr2_send, gr2.at[ring], 11, in_ring(lax.rem(ring + k, N))).start()
    gr2[ring] = part_sum

    ready(an_recv, recv_sem.at[9])
    answer_out[0] = an_send[...].astype(jnp.float32) + an_recv[...].astype(jnp.float32)

    def responder(owner):
        held = jnp.int32(0)
        for d in range(N):
            held = jnp.where(pairing[0, d] == owner, d, held)
        return held

    sources = [responder(along_x(k)) for k in range(4)]
    ready(own_twin, recv_sem.at[4])
    ready(pre_z.at[pl.ds(0, 3)], recv_sem.at[10])
    for k in (2, 1, 3):
        pre_pick[k] = pre_z[sources[k] // 4, lax.rem(sources[k], 4)]
        to(pre_pick.at[k], pre_home.at[x], 12, {"resp": along_x(k)}).start()
    pre_home[x] = pre_z[sources[0] // 4, lax.rem(sources[0], 4)]

    ready(gr2.at[pl.ds(0, 15)], recv_sem.at[11])
    total = (jnp.sum(gr2[...].astype(jnp.float32), axis=0) * scale).astype(jnp.bfloat16)
    gr3_send[...] = total
    for k in PLANE_ORDER:
        peer = (lax.rem(y + k // 4, 4)) * 4 + lax.rem(x + k % 4, 4)
        to(gr3_send, gr3.at[plane], 13, in_plane(peer)).start()
    gr3[plane] = total

    ready(pre_home.at[pl.ds(0, 3)], recv_sem.at[12])
    done = (
        own_proj[rows(f, 64), :]
        + own_twin[...].astype(jnp.float32)
        + pre_home[...].reshape(64, 128).astype(jnp.float32)
    )
    done_half[...] = done
    done_copy = to(done_half, done_twin, 14, twin)
    done_copy.start()
    prompt_out[0, rows(f, 64), :] = done
    ready(done_twin, recv_sem.at[14])
    prompt_out[0, rows(1 - f, 64), :] = done_twin[...]

    ready(gr3.at[pl.ds(0, 15)], recv_sem.at[13])
    for b in range(4):
        up_out[b // 2, :, (b % 2) * 128:(b % 2) * 128 + 128] = (
            gr3[4 * b:4 * b + 4].reshape(64, 128).astype(jnp.float32)
        )

    ready(mid1.at[pl.ds(0, 11)], send_sem.at[0])
    ready(mid2.at[pl.ds(0, 15)], send_sem.at[2])
    own_copy.wait_send()
    a_copy.wait_send()
    pre_copy.wait_send()
    ready(gr_send.at[pl.ds(0, 15)], send_sem.at[7])
    ready(pre_x.at[pl.ds(0, 3)], send_sem.at[8])
    to_twin.wait_send()
    ready(pre_z.at[pl.ds(0, 3)], send_sem.at[10])
    ready(gr2.at[pl.ds(0, 15)], send_sem.at[11])
    ready(pre_pick.at[pl.ds(0, 3)], send_sem.at[12])
    ready(gr3.at[pl.ds(0, 15)], send_sem.at[13])
    done_copy.wait_send()


def store(a, b, c, a_out, b_out, c_out, sem):
    copies = [pltpu.make_async_copy(*pair, sem.at[i]) for i, pair in enumerate([(a, a_out), (b, b_out), (c, c_out)])]
    for copy in copies:
        copy.start()
    for copy in copies:
        copy.wait()


def on_device(scale, *args):
    bf, f32 = jnp.bfloat16, jnp.float32
    hbm = pl.BlockSpec(memory_space=pltpu.HBM)
    vmem = pl.BlockSpec(memory_space=pltpu.VMEM)
    V = pltpu.VMEM
    args = [pltpu.with_memory_space_constraint(a, pltpu.HBM) for a in args]
    held = pl.pallas_call(
        functools.partial(kernel, scale),
        out_shape=(
            jax.ShapeDtypeStruct((1, 128, 128), f32),
            jax.ShapeDtypeStruct((1, 256, 128), f32),
            jax.ShapeDtypeStruct((2, 64, 256), f32),
        ),
        in_specs=[hbm] * 13,
        out_specs=(vmem, vmem, vmem),
        scratch_shapes=[
            V((128, 2048), bf), V((128, 256), bf), V((128, 256), bf), V((128, 128), bf), V((128, 2048), bf),
            V((256, 2048), bf), V((256, 256), bf), V((256, 256), bf), V((256, 128), bf), V((256, 2048), bf),
            V((2, 64, 256), bf), pltpu.SMEM((1, 2), jnp.int32), pltpu.SMEM((1, 16), jnp.int32),
            V((128, 512), bf), V((36, 16, 128), bf), V((256, 512), bf), V((36, 16, 128), bf),
            V((16, 3, 16, 128), bf), V((16, 3, 16, 128), bf), V((16, 3, 16, 128), bf), V((128, 128), bf),
            V((128, 384), bf), V((4, 128, 1024), f32), V((4, 128, 1024), f32), V((4, 8, 1024), f32),
            V((2, 256, 1024), bf), V((2, 256, 1024), bf), V((512, 512), bf), V((128, 128), f32), V((128, 512), f32),
            V((64, 128), bf), V((64, 128), bf), V((128, 128), f32), V((64, 128), bf), V((2, 64, 128), bf),
            V((4, 16, 128), bf), V((4, 4, 16, 128), bf), V((4, 16, 128), bf), V((4, 16, 128), bf),
            V((64, 128), f32), V((64, 128), f32),
            V((256, 128), bf), V((256, 128), bf),
            V((16, 16, 128), bf), V((16, 16, 128), bf), V((16, 128), bf), V((16, 16, 128), bf),
            V((16, 128), bf), V((16, 16, 128), bf),
            pltpu.SemaphoreType.DMA((13,)), pltpu.SemaphoreType.DMA((15,)), pltpu.SemaphoreType.DMA((15,)),
        ],
        compiler_params=pltpu.CompilerParams(
            collective_id=0, has_side_effects=True, vmem_limit_bytes=48 * 1024 * 1024
        ),
        name="adapter_backward",
    )(*args)
    return pl.pallas_call(
        store,
        out_shape=tuple(jax.ShapeDtypeStruct(h.shape, h.dtype) for h in held),
        in_specs=[pl.BlockSpec(memory_space=pl.ANY)] * 3,
        out_specs=(pl.BlockSpec(memory_space=pl.ANY),) * 3,
        scratch_shapes=[pltpu.SemaphoreType.DMA((3,))],
        compiler_params=pltpu.CompilerParams(vmem_limit_bytes=65136 * 1024),
        name="store",
    )(*[pltpu.with_memory_space_constraint(h, pltpu.VMEM) for h in held])


def solution(mesh):
    rows = ("prompt", "resp")
    wide = P(rows, None, "fsdp")
    whole = P(rows, None, None)
    scale = 1.0 / math.sqrt(mesh.shape["prompt"] * mesh.shape["resp"] * 2 * T)
    return jax.shard_map(
        functools.partial(on_device, scale),
        mesh=mesh,
        in_specs=(
            wide, wide, wide, whole, wide, wide, wide, wide, whole, wide,
            P(None, None, "fsdp"), P(rows, None), P("prompt", None),
        ),
        out_specs=(whole, whole, P(None, None, "fsdp")),
        check_vma=False,
    )
```

```python
import functools
import math

import jax
import jax.numpy as jnp
from jax import lax
from jax.experimental import pallas as pl
from jax.experimental.pallas import tpu as pltpu
from jax.sharding import PartitionSpec as P

MESH = pl.DeviceIdType.MESH
HD = 128
T = 128
N = 16
NT = (((1,), (1,)), ((), ()))
TN = (((0,), (0,)), ((), ()))
NN = (((1,), (0,)), ((), ()))
FACTOR = 1.0 / math.sqrt(HD)
EXP2_FACTOR = FACTOR * math.log2(math.e)
SHIFTS = (0, 1, 3)
NEAR_ORDER = ((1, 2), (2, 2), (1, 1), (2, 1), (1, 3), (2, 3), (1, 0), (2, 0), (0, 2), (0, 1), (0, 3))
RESP_ORDER = (10, 9, 11, 8, 6, 14, 5, 7, 13, 15, 4, 12, 2, 1, 3)
PLANE_ORDER = (10, 9, 11, 6, 14, 8, 2, 5, 7, 13, 15, 4, 12, 1, 3)
RING_ORDER = (8, 7, 9, 6, 10, 5, 11, 4, 12, 3, 13, 2, 14, 1, 15)


def mm(a, b, dims):
    return lax.dot_general(a, b, dims, preferred_element_type=jnp.float32)


def ready(ref, sem):
    pltpu.make_async_copy(ref, ref, sem).wait()


def backward_tile(keys, values, queries, grads, visible, live, prefix):
    scores = mm(keys, queries, NT)
    dprobs = mm(values, grads, NT)
    own = jnp.where(visible, scores[prefix:], -1e30)
    highest = jnp.max(own, axis=0, keepdims=True)
    if prefix:
        highest = jnp.maximum(highest, jnp.max(scores[:prefix], axis=0, keepdims=True))
        scores = jnp.concatenate([scores[:prefix], own], axis=0)
    else:
        scores = own
    weights = jnp.exp2((scores - highest) * EXP2_FACTOR)
    inverse = 1.0 / jnp.sum(weights, axis=0, keepdims=True)
    if live is not None:
        inverse = jnp.where(live, inverse, 0.0)
    probs = weights * inverse
    delta = jnp.sum(probs * dprobs, axis=0, keepdims=True)
    dscores = probs * (dprobs - delta)
    return probs.astype(jnp.bfloat16), dscores.astype(jnp.bfloat16)


def joined_tile(keys, values, queries, grads, own_weights, own_dprobs, own_stats, live):
    scores = mm(keys, queries, NT)
    dprobs = mm(values, grads, NT)
    own_highest, own_sum, own_dot = own_stats[0:1], own_stats[1:2], own_stats[2:3]
    highest = jnp.maximum(own_highest, jnp.max(scores, axis=0, keepdims=True))
    weights = jnp.exp2((scores - highest) * EXP2_FACTOR)
    rescale = jnp.exp2((own_highest - highest) * EXP2_FACTOR)
    total = own_sum * rescale + jnp.sum(weights, axis=0, keepdims=True)
    inverse = jnp.where(live, 1.0 / total, 0.0)
    delta = (own_dot * rescale + jnp.sum(weights * dprobs, axis=0, keepdims=True)) * inverse
    probs = weights * inverse
    own_probs = own_weights * (rescale * inverse)
    return (
        probs.astype(jnp.bfloat16),
        (probs * (dprobs - delta)).astype(jnp.bfloat16),
        own_probs.astype(jnp.bfloat16),
        (own_probs * (own_dprobs - delta)).astype(jnp.bfloat16),
    )


def kernel(
    scale,
    pq_h, pk_h, pv_h, pa_h, pg_h, aq_h, ak_h, av_h, aa_h, ag_h, up_h, lens_h, pairing_h,
    prompt_out, answer_out, up_out,
    pq, pk, pv, pa, pg, aq, ak, av, aa, ag, up, lens, pairing,
    wide_up, pack, kv_slot, pre, mid1, mid2, got, a_pre, a_cols, own_w, own_dp, own_st,
    probs_s, dsc_s, dkv, own_proj, outer_acc,
    own_half, own_twin, pre_part, pre_twin, pre_half, pre_z, pre_pick, pre_home, done_half, done_twin,
    an_send, an_recv, gr_send, gr1, gr2_send, gr2, gr3_send, gr3,
    load_sem, send_sem, recv_sem,
):
    f = lax.axis_index("fsdp")
    p = lax.axis_index("prompt")
    r = lax.axis_index("resp")
    twin = {"fsdp": 1 - f}
    x, z_hi = lax.rem(r, 4), r // 4
    y, z_lo = p // 4, lax.rem(p, 4)
    plane = y * 4 + x
    ring = z_hi * 4 + z_lo

    def in_plane(at):
        return {"prompt": (at // 4) * 4 + z_lo, "resp": z_hi * 4 + lax.rem(at, 4)}

    def in_ring(at):
        return {"prompt": y * 4 + lax.rem(at, 4), "resp": (at // 4) * 4 + x}

    def along_x(k):
        return z_hi * 4 + lax.rem(x + k, 4)

    def along_z(k):
        return lax.rem(z_hi + k, 4) * 4 + x

    barrier = pltpu.get_barrier_semaphore()

    def greet(where):
        pl.semaphore_signal(barrier, inc=1, device_id=where, device_id_type=MESH)

    for shift, k in NEAR_ORDER:
        greet({"resp": lax.rem(z_hi + SHIFTS[shift], 4) * 4 + lax.rem(x + k, 4)})

    loads = [
        pltpu.make_async_copy(src.at[0] if lead else src, dst, load_sem.at[i])
        for i, (src, dst, lead) in enumerate([
            (up_h, up, False), (pa_h, pa, True), (pk_h, pk, True), (pv_h, pv, True),
            (pq_h, pq, True), (pg_h, pg, True), (aa_h, aa, True), (ak_h, ak, True),
            (av_h, av, True), (aq_h, aq, True), (ag_h, ag, True), (lens_h, lens, False), (pairing_h, pairing, False),
        ])
    ]
    for load in loads:
        load.start()

    greet(twin)
    for k in range(4, N):
        greet({"prompt": (lax.rem(y + k // 4, 4)) * 4 + z_lo, "resp": along_x(k % 4)})
    for k in range(1, 4):
        greet({"prompt": y * 4 + lax.rem(z_lo + k, 4)})

    wide_up[...] = jnp.zeros_like(wide_up)
    for load in loads[:4]:
        load.wait()
    wide_up[0:64, 0:256] = up[0]
    wide_up[64:128, 256:512] = up[1]
    lifted = mm(pa[...], wide_up[...], NN)
    for i, base in enumerate((pk, pv)):
        full = (base[...].astype(jnp.float32) + lifted[:, 256 * i:256 * i + 256]).astype(jnp.bfloat16)
        for h in range(2):
            pack[16 * i + 8 * h:16 * i + 8 * h + 8] = full[:, h * HD:(h + 1) * HD].reshape(8, 16, HD)
    pack[32:36] = pa[pl.ds(pl.multiple_of(f * 64, 64), 64), :].reshape(4, 16, HD)

    pl.semaphore_wait(barrier, 27)

    def to(src, dst, lane, where):
        return pltpu.make_async_remote_copy(
            src_ref=src, dst_ref=dst, send_sem=send_sem.at[lane], recv_sem=recv_sem.at[lane],
            device_id=where, device_id_type=MESH,
        )

    def rows(index, size=16):
        return pl.ds(pl.multiple_of(index * size, size), size)

    for shift, k in NEAR_ORDER:
        peer_x = lax.rem(x + k, 4)
        peer = lax.rem(z_hi + SHIFTS[shift], 4) * 4 + peer_x
        to(pack.at[pl.ds(3 * (4 * shift + peer_x), 3)], mid1.at[r], 0, {"resp": peer}).start()
    mid1[r] = pack[pl.ds(3 * x, 3)]
    for k in range(4):
        mid1[lax.rem(z_hi + 2, 4) * 4 + k] = jnp.zeros((3, 16, HD), jnp.bfloat16)

    lane_at = lax.rem(lax.broadcasted_iota(jnp.int32, (T, 256), 1), T)
    visible = lax.broadcasted_iota(jnp.int32, (T, 256), 0) <= lane_at
    loads[4].wait()
    loads[5].wait()

    def own_head(h, carry):
        at = pl.multiple_of(h * HD, HD)
        keys = pack[pl.ds(8 * h, 8)].reshape(T, HD)
        values = pack[pl.ds(16 + 8 * h, 8)].reshape(T, HD)

        def heads(ref, g, count):
            return jnp.concatenate(
                [ref[:, pl.ds(pl.multiple_of(h * 1024 + (g + i) * HD, HD), HD)] for i in range(count)], axis=0
            )

        for g in range(0, 8, 2):
            probs, dscores = backward_tile(keys, values, heads(pq, g, 2), heads(pg, g, 2), visible, None, 0)
            probs_s[0, 0:128, g * HD:(g + 2) * HD] = probs
            dsc_s[0, 0:128, g * HD:(g + 2) * HD] = dscores
        dkv[0:128, pl.ds(at, HD)] = (mm(dsc_s[0, 0:128, :], heads(pq, 0, 8), NN) * FACTOR).astype(jnp.bfloat16)
        dkv[0:128, pl.ds(pl.multiple_of(256 + h * HD, HD), HD)] = mm(
            probs_s[0, 0:128, :], heads(pg, 0, 8), NN
        ).astype(jnp.bfloat16)
        return carry

    lax.fori_loop(0, 2, own_head, 0)

    loads[12].wait()
    ready(mid1.at[pl.ds(0, 11)], recv_sem.at[0])

    def held_of(member):
        owner = pairing[0, member]
        return jnp.where(lax.rem(owner // 4 + 6 - z_hi, 4) == 0, r, owner)

    for k in RESP_ORDER:
        peer = lax.rem(r + k, N)
        mid2[peer] = mid1[held_of(peer)]
        to(mid2.at[peer], got.at[r], 2, {"resp": peer}).start()
    got[r] = mid1[held_of(r)]

    own_proj[...] = mm(dkv[0:128, :], wide_up[...], NT)
    own_half[...] = own_proj[rows(1 - f, 64), :].astype(jnp.bfloat16)
    own_copy = to(own_half, own_twin, 4, twin)
    own_copy.start()
    for load in loads[6:12]:
        load.wait()
    lifted_slots = mm(aa[...], wide_up[...], NN)
    kv_slot[:, 0:256] = (ak[...].astype(jnp.float32) + lifted_slots[:, 0:256]).astype(jnp.bfloat16)
    kv_slot[:, 256:512] = (av[...].astype(jnp.float32) + lifted_slots[:, 256:512]).astype(jnp.bfloat16)
    outer_acc[...] = mm(pa[...], dkv[0:128, :], TN)
    a_cols[:, 128:256] = jnp.transpose(aa[0:128, :])
    a_cols[:, 256:384] = jnp.transpose(aa[128:256, :])

    row_at = lax.rem(lax.broadcasted_iota(jnp.int32, (1, 256), 1), T)

    def heads(ref, c, h, g, count):
        return jnp.concatenate(
            [ref[c * T:(c + 1) * T, (8 * h + g + i) * HD:(8 * h + g + i + 1) * HD] for i in range(count)], axis=0
        )

    for h in range(2):
        for c in range(2):
            keys = kv_slot[c * T:(c + 1) * T, h * HD:(h + 1) * HD]
            values = kv_slot[c * T:(c + 1) * T, 256 + h * HD:256 + (h + 1) * HD]
            for g in range(0, 8, 2):
                cols = slice(g * HD, (g + 2) * HD)
                scores = jnp.where(visible, mm(keys, heads(aq, c, h, g, 2), NT), -1e30)
                dprobs = mm(values, heads(ag, c, h, g, 2), NT)
                highest = jnp.max(scores, axis=0, keepdims=True)
                weights = jnp.exp2((scores - highest) * EXP2_FACTOR)
                own_w[2 * h + c, :, cols] = weights
                own_dp[2 * h + c, :, cols] = dprobs
                own_st[2 * h + c, 0:1, cols] = highest
                own_st[2 * h + c, 1:2, cols] = jnp.sum(weights, axis=0, keepdims=True)
                own_st[2 * h + c, 2:3, cols] = jnp.sum(weights * dprobs, axis=0, keepdims=True)

    def slot_head(h):
        key_cols = slice(h * HD, (h + 1) * HD)
        value_cols = slice(256 + h * HD, 256 + (h + 1) * HD)
        keys = pre[8 * h:8 * h + 8].reshape(T, HD)
        values = pre[16 + 8 * h:24 + 8 * h].reshape(T, HD)
        key_sum, value_sum = 0.0, 0.0
        for c in range(2):
            live = row_at < lens[0, c]
            for g in range(0, 8, 2):
                cols = slice(g * HD, (g + 2) * HD)
                probs, dscores, own_probs, own_dscores = joined_tile(
                    keys, values, heads(aq, c, h, g, 2), heads(ag, c, h, g, 2),
                    own_w[2 * h + c, :, cols], own_dp[2 * h + c, :, cols], own_st[2 * h + c, :, cols], live,
                )
                probs_s[c, 0:128, cols] = probs
                probs_s[c, 128:256, cols] = own_probs
                dsc_s[c, 0:128, cols] = dscores
                dsc_s[c, 128:256, cols] = own_dscores
            key_grad = mm(dsc_s[c], heads(aq, c, h, 0, 8), NN) * FACTOR
            value_grad = mm(probs_s[c], heads(ag, c, h, 0, 8), NN)
            dkv[256 + c * T:256 + (c + 1) * T, key_cols] = key_grad[T:].astype(jnp.bfloat16)
            dkv[256 + c * T:256 + (c + 1) * T, value_cols] = value_grad[T:].astype(jnp.bfloat16)
            key_sum = key_sum + key_grad[:T]
            value_sum = value_sum + value_grad[:T]
        dkv[128:256, key_cols] = key_sum.astype(jnp.bfloat16)
        dkv[128:256, value_cols] = value_sum.astype(jnp.bfloat16)

    ready(got.at[pl.ds(0, 15)], recv_sem.at[2])
    from_plane = pairing[0, r] // 4
    for shift in range(3):
        for k in range(4):
            at = 3 * (4 * shift + k)
            pre[at:at + 3] = got[lax.rem(from_plane + SHIFTS[shift], 4) * 4 + k]

    a_pre[rows(f, 64), :] = pre[32:36].reshape(64, HD)
    a_copy = to(a_pre.at[rows(f, 64)], a_pre.at[rows(f, 64)], 5, twin)
    a_copy.start()
    slot_head(0)
    slot_head(1)

    ready(a_pre.at[pl.ds(0, 64)], recv_sem.at[5])
    a_cols[:, 0:128] = jnp.transpose(a_pre[...])
    for b, (row, col) in enumerate([(0, 0), (0, 128), (64, 256), (64, 384)]):
        block = outer_acc[row:row + 64, col:col + 128] + mm(
            a_cols[row:row + 64, :], dkv[128:512, col:col + 128], NN
        )
        gr_send[4 * b:4 * b + 4] = block.astype(jnp.bfloat16).reshape(4, 16, 128)
    for k in PLANE_ORDER:
        peer = (lax.rem(y + k // 4, 4)) * 4 + lax.rem(x + k % 4, 4)
        to(gr_send.at[peer], gr1.at[plane], 7, in_plane(peer)).start()
    gr1[plane] = gr_send[plane]

    pre_part[...] = mm(dkv[128:256, :], wide_up[...], NT)
    pre_half[0] = pre_part[rows(1 - f, 64), :].astype(jnp.bfloat16)
    pre_copy = to(pre_half.at[0], pre_twin, 6, twin)
    pre_copy.start()

    an_send[...] = mm(dkv[256:512, :], wide_up[...], NT).astype(jnp.bfloat16)
    to_twin = to(an_send, an_recv, 9, twin)

    ready(pre_twin, recv_sem.at[6])
    both = (pre_part[rows(f, 64), :] + pre_twin[...].astype(jnp.float32)).astype(jnp.bfloat16)
    pre_half[1] = both
    for k in (2, 1, 3):
        to(pre_half.at[1], pre_z.at[z_hi], 10, {"resp": along_z(k)}).start()
    pre_z[z_hi] = both
    to_twin.start()

    ready(gr1.at[pl.ds(0, 15)], recv_sem.at[7])
    part_sum = jnp.sum(gr1[...].astype(jnp.float32), axis=0).astype(jnp.bfloat16)
    gr2_send[...] = part_sum
    for k in RING_ORDER:
        to(gr2_send, gr2.at[ring], 11, in_ring(lax.rem(ring + k, N))).start()
    gr2[ring] = part_sum

    ready(an_recv, recv_sem.at[9])
    answer_out[0] = an_send[...].astype(jnp.float32) + an_recv[...].astype(jnp.float32)

    def responder(owner):
        held = jnp.int32(0)
        for d in range(N):
            held = jnp.where(pairing[0, d] == owner, d, held)
        return held

    sources = [responder(along_x(k)) for k in range(4)]
    ready(own_twin, recv_sem.at[4])
    ready(pre_z.at[pl.ds(0, 3)], recv_sem.at[10])
    for k in (2, 1, 3, 0):
        mine = pre_z[jnp.where(lax.rem(sources[k], 4) == x, sources[k] // 4, z_hi)]
        if k:
            pre_pick[k] = mine
            to(pre_pick.at[k], pre_home.at[x], 12, {"resp": along_x(k)}).start()
        else:
            pre_home[x] = mine

    ready(gr2.at[pl.ds(0, 15)], recv_sem.at[11])
    total = (jnp.sum(gr2[...].astype(jnp.float32), axis=0) * scale).astype(jnp.bfloat16)
    gr3_send[...] = total
    for k in PLANE_ORDER:
        peer = (lax.rem(y + k // 4, 4)) * 4 + lax.rem(x + k % 4, 4)
        to(gr3_send, gr3.at[plane], 13, in_plane(peer)).start()
    gr3[plane] = total

    ready(pre_home.at[pl.ds(0, 3)], recv_sem.at[12])
    done = (
        own_proj[rows(f, 64), :]
        + own_twin[...].astype(jnp.float32)
        + pre_home[lax.rem(sources[0], 4)].astype(jnp.float32)
    )
    done_half[...] = done
    done_copy = to(done_half, done_twin, 14, twin)
    done_copy.start()
    prompt_out[0, rows(f, 64), :] = done
    ready(done_twin, recv_sem.at[14])
    prompt_out[0, rows(1 - f, 64), :] = done_twin[...]

    ready(gr3.at[pl.ds(0, 15)], recv_sem.at[13])
    for b in range(4):
        up_out[b // 2, :, (b % 2) * 128:(b % 2) * 128 + 128] = (
            gr3[4 * b:4 * b + 4].reshape(64, 128).astype(jnp.float32)
        )

    ready(mid1.at[pl.ds(0, 11)], send_sem.at[0])
    ready(mid2.at[pl.ds(0, 15)], send_sem.at[2])
    own_copy.wait_send()
    a_copy.wait_send()
    pre_copy.wait_send()
    ready(gr_send.at[pl.ds(0, 15)], send_sem.at[7])
    to_twin.wait_send()
    ready(pre_z.at[pl.ds(0, 3)], send_sem.at[10])
    ready(gr2.at[pl.ds(0, 15)], send_sem.at[11])
    ready(pre_pick.at[pl.ds(0, 3)], send_sem.at[12])
    ready(gr3.at[pl.ds(0, 15)], send_sem.at[13])
    done_copy.wait_send()


def store(a, b, c, a_out, b_out, c_out, sem):
    copies = [pltpu.make_async_copy(*pair, sem.at[i]) for i, pair in enumerate([(a, a_out), (b, b_out), (c, c_out)])]
    for copy in copies:
        copy.start()
    for copy in copies:
        copy.wait()


def on_device(scale, *args):
    bf, f32 = jnp.bfloat16, jnp.float32
    hbm = pl.BlockSpec(memory_space=pltpu.HBM)
    vmem = pl.BlockSpec(memory_space=pltpu.VMEM)
    V = pltpu.VMEM
    args = [pltpu.with_memory_space_constraint(a, pltpu.HBM) for a in args]
    held = pl.pallas_call(
        functools.partial(kernel, scale),
        out_shape=(
            jax.ShapeDtypeStruct((1, 128, 128), f32),
            jax.ShapeDtypeStruct((1, 256, 128), f32),
            jax.ShapeDtypeStruct((2, 64, 256), f32),
        ),
        in_specs=[hbm] * 13,
        out_specs=(vmem, vmem, vmem),
        scratch_shapes=[
            V((128, 2048), bf), V((128, 256), bf), V((128, 256), bf), V((128, 128), bf), V((128, 2048), bf),
            V((256, 2048), bf), V((256, 256), bf), V((256, 256), bf), V((256, 128), bf), V((256, 2048), bf),
            V((2, 64, 256), bf), pltpu.SMEM((1, 2), jnp.int32), pltpu.SMEM((1, 16), jnp.int32),
            V((128, 512), bf), V((36, 16, 128), bf), V((256, 512), bf), V((36, 16, 128), bf),
            V((16, 3, 16, 128), bf), V((16, 3, 16, 128), bf), V((16, 3, 16, 128), bf), V((128, 128), bf),
            V((128, 384), bf), V((4, 128, 1024), f32), V((4, 128, 1024), f32), V((4, 8, 1024), f32),
            V((2, 256, 1024), bf), V((2, 256, 1024), bf), V((512, 512), bf), V((128, 128), f32), V((128, 512), f32),
            V((64, 128), bf), V((64, 128), bf), V((128, 128), f32), V((64, 128), bf), V((2, 64, 128), bf),
            V((4, 64, 128), bf), V((4, 64, 128), bf), V((4, 64, 128), bf),
            V((64, 128), f32), V((64, 128), f32),
            V((256, 128), bf), V((256, 128), bf),
            V((16, 16, 128), bf), V((16, 16, 128), bf), V((16, 128), bf), V((16, 16, 128), bf),
            V((16, 128), bf), V((16, 16, 128), bf),
            pltpu.SemaphoreType.DMA((13,)), pltpu.SemaphoreType.DMA((15,)), pltpu.SemaphoreType.DMA((15,)),
        ],
        compiler_params=pltpu.CompilerParams(
            collective_id=0, has_side_effects=True, vmem_limit_bytes=48 * 1024 * 1024
        ),
        name="adapter_backward",
    )(*args)
    return pl.pallas_call(
        store,
        out_shape=tuple(jax.ShapeDtypeStruct(h.shape, h.dtype) for h in held),
        in_specs=[pl.BlockSpec(memory_space=pl.ANY)] * 3,
        out_specs=(pl.BlockSpec(memory_space=pl.ANY),) * 3,
        scratch_shapes=[pltpu.SemaphoreType.DMA((3,))],
        compiler_params=pltpu.CompilerParams(vmem_limit_bytes=65136 * 1024),
        name="store",
    )(*[pltpu.with_memory_space_constraint(h, pltpu.VMEM) for h in held])


def solution(mesh):
    rows = ("prompt", "resp")
    wide = P(rows, None, "fsdp")
    whole = P(rows, None, None)
    scale = 1.0 / math.sqrt(mesh.shape["prompt"] * mesh.shape["resp"] * 2 * T)
    return jax.shard_map(
        functools.partial(on_device, scale),
        mesh=mesh,
        in_specs=(
            wide, wide, wide, whole, wide, wide, wide, wide, whole, wide,
            P(None, None, "fsdp"), P(rows, None), P("prompt", None),
        ),
        out_specs=(whole, whole, P(None, None, "fsdp")),
        check_vma=False,
    )
```

```python
import functools
import math

import jax
import jax.numpy as jnp
from jax import lax
from jax.experimental import pallas as pl
from jax.experimental.pallas import tpu as pltpu
from jax.sharding import PartitionSpec as P

MESH = pl.DeviceIdType.MESH
HD = 128
T = 128
N = 16
NT = (((1,), (1,)), ((), ()))
TN = (((0,), (0,)), ((), ()))
NN = (((1,), (0,)), ((), ()))
FACTOR = 1.0 / math.sqrt(HD)
EXP2_FACTOR = FACTOR * math.log2(math.e)
SHIFTS = (0, 1, 3)
NEAR_ORDER = ((1, 2), (2, 2), (1, 1), (2, 1), (1, 3), (2, 3), (1, 0), (2, 0), (0, 2), (0, 1), (0, 3))
RESP_ORDER = (10, 9, 11, 8, 6, 14, 5, 7, 13, 15, 4, 12, 2, 1, 3)
PLANE_ORDER = (10, 9, 11, 6, 14, 8, 2, 5, 7, 13, 15, 4, 12, 1, 3)
RING_ORDER = (8, 7, 9, 6, 10, 5, 11, 4, 12, 3, 13, 2, 14, 1, 15)


def mm(a, b, dims):
    return lax.dot_general(a, b, dims, preferred_element_type=jnp.float32)


def ready(ref, sem):
    pltpu.make_async_copy(ref, ref, sem).wait()


def backward_tile(keys, values, queries, grads, visible, live, prefix):
    scores = mm(keys, queries, NT)
    dprobs = mm(values, grads, NT)
    own = jnp.where(visible, scores[prefix:], -1e30)
    highest = jnp.max(own, axis=0, keepdims=True)
    if prefix:
        highest = jnp.maximum(highest, jnp.max(scores[:prefix], axis=0, keepdims=True))
        scores = jnp.concatenate([scores[:prefix], own], axis=0)
    else:
        scores = own
    weights = jnp.exp2((scores - highest) * EXP2_FACTOR)
    inverse = 1.0 / jnp.sum(weights, axis=0, keepdims=True)
    if live is not None:
        inverse = jnp.where(live, inverse, 0.0)
    probs = weights * inverse
    delta = jnp.sum(probs * dprobs, axis=0, keepdims=True)
    dscores = probs * (dprobs - delta)
    return probs.astype(jnp.bfloat16), dscores.astype(jnp.bfloat16)


def joined_tile(keys, values, queries, grads, own_weights, own_dprobs, own_stats, live):
    scores = mm(keys, queries, NT)
    dprobs = mm(values, grads, NT)
    own_highest, own_sum, own_dot = own_stats[0:1], own_stats[1:2], own_stats[2:3]
    highest = jnp.maximum(own_highest, jnp.max(scores, axis=0, keepdims=True))
    weights = jnp.exp2((scores - highest) * EXP2_FACTOR)
    rescale = jnp.exp2((own_highest - highest) * EXP2_FACTOR)
    total = own_sum * rescale + jnp.sum(weights, axis=0, keepdims=True)
    inverse = jnp.where(live, 1.0 / total, 0.0)
    delta = (own_dot * rescale + jnp.sum(weights * dprobs, axis=0, keepdims=True)) * inverse
    probs = weights * inverse
    own_probs = own_weights * (rescale * inverse)
    return (
        probs.astype(jnp.bfloat16),
        (probs * (dprobs - delta)).astype(jnp.bfloat16),
        own_probs.astype(jnp.bfloat16),
        (own_probs * (own_dprobs - delta)).astype(jnp.bfloat16),
    )


def kernel(
    scale,
    pq_h, pk_h, pv_h, pa_h, pg_h, aq_h, ak_h, av_h, aa_h, ag_h, up_h, lens_h, pairing_h,
    prompt_out, answer_out, up_out,
    pq, pk, pv, pa, pg, aq, ak, av, aa, ag, up, lens, pairing,
    wide_up, pack, parcel, kv_slot, pre, pre2, mid1, mid2, got, got2, a_pre, a_cols, own_w, own_dp, own_st,
    probs_s, dsc_s, dkv, own_proj, outer_acc,
    own_half, own_twin, pre_part, pre_twin, pre_half, pre_z, pre_pick, pre_home, done_half, done_twin,
    an_send, an_recv, gr_send, gr1, gr2_send, gr2, gr3_send, gr3,
    load_sem, send_sem, recv_sem,
):
    f = lax.axis_index("fsdp")
    p = lax.axis_index("prompt")
    r = lax.axis_index("resp")
    twin = {"fsdp": 1 - f}
    x, z_hi = lax.rem(r, 4), r // 4
    y, z_lo = p // 4, lax.rem(p, 4)
    plane = y * 4 + x
    ring = z_hi * 4 + z_lo

    def in_plane(at):
        return {"prompt": (at // 4) * 4 + z_lo, "resp": z_hi * 4 + lax.rem(at, 4)}

    def in_ring(at):
        return {"prompt": y * 4 + lax.rem(at, 4), "resp": (at // 4) * 4 + x}

    def along_x(k):
        return z_hi * 4 + lax.rem(x + k, 4)

    def along_z(k):
        return lax.rem(z_hi + k, 4) * 4 + x

    barrier = pltpu.get_barrier_semaphore()

    def greet(where):
        pl.semaphore_signal(barrier, inc=1, device_id=where, device_id_type=MESH)

    for shift, k in NEAR_ORDER:
        greet({"resp": lax.rem(z_hi + SHIFTS[shift], 4) * 4 + lax.rem(x + k, 4)})

    loads = [
        pltpu.make_async_copy(src.at[0] if lead else src, dst, load_sem.at[i])
        for i, (src, dst, lead) in enumerate([
            (up_h, up, False), (pa_h, pa, True), (pk_h, pk, True), (pv_h, pv, True),
            (pq_h, pq, True), (pg_h, pg, True), (aa_h, aa, True), (ak_h, ak, True),
            (av_h, av, True), (aq_h, aq, True), (ag_h, ag, True), (lens_h, lens, False), (pairing_h, pairing, False),
        ])
    ]
    for load in loads:
        load.start()

    greet(twin)
    for k in range(4, N):
        greet({"prompt": (lax.rem(y + k // 4, 4)) * 4 + z_lo, "resp": along_x(k % 4)})
    for k in range(1, 4):
        greet({"prompt": y * 4 + lax.rem(z_lo + k, 4)})

    wide_up[...] = jnp.zeros_like(wide_up)
    for load in loads[:4]:
        load.wait()
    wide_up[0:64, 0:256] = up[0]
    wide_up[64:128, 256:512] = up[1]
    lifted = mm(pa[...], wide_up[...], NN)
    for i, base in enumerate((pk, pv)):
        full = (base[...].astype(jnp.float32) + lifted[:, 256 * i:256 * i + 256]).astype(jnp.bfloat16)
        for h in range(2):
            pack[16 * i + 8 * h:16 * i + 8 * h + 8] = full[:, h * HD:(h + 1) * HD].reshape(8, 16, HD)
    for i, tiles in enumerate((0, 16, 8)):
        parcel[4 * i:4 * i + 4, 0:2] = pack[tiles:tiles + 8].reshape(4, 2, 16, HD)
    parcel[0:8, 2] = pack[24:32]
    parcel[8:12, 2] = pa[pl.ds(pl.multiple_of(f * 64, 64), 64), :].reshape(4, 16, HD)

    pl.semaphore_wait(barrier, 27)

    def to(src, dst, lane, where):
        return pltpu.make_async_remote_copy(
            src_ref=src, dst_ref=dst, send_sem=send_sem.at[lane], recv_sem=recv_sem.at[lane],
            device_id=where, device_id_type=MESH,
        )

    def rows(index, size=16):
        return pl.ds(pl.multiple_of(index * size, size), size)

    for shift, k in NEAR_ORDER:
        peer_x = lax.rem(x + k, 4)
        peer = lax.rem(z_hi + SHIFTS[shift], 4) * 4 + peer_x
        to(parcel.at[4 * shift + peer_x], mid1.at[r], 0, {"resp": peer}).start()
    mid1[r] = parcel[x]
    for k in range(4):
        mid1[lax.rem(z_hi + 2, 4) * 4 + k] = jnp.zeros((3, 16, HD), jnp.bfloat16)

    lane_at = lax.rem(lax.broadcasted_iota(jnp.int32, (T, 256), 1), T)
    visible = lax.broadcasted_iota(jnp.int32, (T, 256), 0) <= lane_at
    loads[4].wait()
    loads[5].wait()

    def own_head(h, carry):
        at = pl.multiple_of(h * HD, HD)
        keys = pack[pl.ds(8 * h, 8)].reshape(T, HD)
        values = pack[pl.ds(16 + 8 * h, 8)].reshape(T, HD)

        def heads(ref, g, count):
            return jnp.concatenate(
                [ref[:, pl.ds(pl.multiple_of(h * 1024 + (g + i) * HD, HD), HD)] for i in range(count)], axis=0
            )

        for g in range(0, 8, 2):
            probs, dscores = backward_tile(keys, values, heads(pq, g, 2), heads(pg, g, 2), visible, None, 0)
            probs_s[0, 0:128, g * HD:(g + 2) * HD] = probs
            dsc_s[0, 0:128, g * HD:(g + 2) * HD] = dscores
        dkv[0:128, pl.ds(at, HD)] = (mm(dsc_s[0, 0:128, :], heads(pq, 0, 8), NN) * FACTOR).astype(jnp.bfloat16)
        dkv[0:128, pl.ds(pl.multiple_of(256 + h * HD, HD), HD)] = mm(
            probs_s[0, 0:128, :], heads(pg, 0, 8), NN
        ).astype(jnp.bfloat16)
        return carry

    lax.fori_loop(0, 2, own_head, 0)

    loads[12].wait()
    ready(mid1.at[pl.ds(0, 11)], recv_sem.at[0])

    def held_of(member):
        owner = pairing[0, member]
        return jnp.where(lax.rem(owner // 4 + 6 - z_hi, 4) == 0, r, owner)

    for k in RESP_ORDER:
        peer = lax.rem(r + k, N)
        mid2[peer] = mid1[held_of(peer)]
        to(mid2.at[peer, pl.ds(0, 2)], got.at[r], 2, {"resp": peer}).start()
    for k in RESP_ORDER:
        peer = lax.rem(r + k, N)
        to(mid2.at[peer, 2], got2.at[r], 3, {"resp": peer}).start()
    mine = mid1[held_of(r)]
    got[r] = mine[0:2]
    got2[r] = mine[2]

    own_proj[...] = mm(dkv[0:128, :], wide_up[...], NT)
    own_half[...] = own_proj[rows(1 - f, 64), :].astype(jnp.bfloat16)
    own_copy = to(own_half, own_twin, 4, twin)
    own_copy.start()
    for load in loads[6:12]:
        load.wait()
    lifted_slots = mm(aa[...], wide_up[...], NN)
    kv_slot[:, 0:256] = (ak[...].astype(jnp.float32) + lifted_slots[:, 0:256]).astype(jnp.bfloat16)
    kv_slot[:, 256:512] = (av[...].astype(jnp.float32) + lifted_slots[:, 256:512]).astype(jnp.bfloat16)
    outer_acc[...] = mm(pa[...], dkv[0:128, :], TN)
    a_cols[:, 128:256] = jnp.transpose(aa[0:128, :])
    a_cols[:, 256:384] = jnp.transpose(aa[128:256, :])

    row_at = lax.rem(lax.broadcasted_iota(jnp.int32, (1, 256), 1), T)

    def heads(ref, c, h, g, count):
        return jnp.concatenate(
            [ref[c * T:(c + 1) * T, (8 * h + g + i) * HD:(8 * h + g + i + 1) * HD] for i in range(count)], axis=0
        )

    for h in range(2):
        for c in range(2):
            keys = kv_slot[c * T:(c + 1) * T, h * HD:(h + 1) * HD]
            values = kv_slot[c * T:(c + 1) * T, 256 + h * HD:256 + (h + 1) * HD]
            for g in range(0, 8, 2):
                cols = slice(g * HD, (g + 2) * HD)
                scores = jnp.where(visible, mm(keys, heads(aq, c, h, g, 2), NT), -1e30)
                dprobs = mm(values, heads(ag, c, h, g, 2), NT)
                highest = jnp.max(scores, axis=0, keepdims=True)
                weights = jnp.exp2((scores - highest) * EXP2_FACTOR)
                own_w[2 * h + c, :, cols] = weights
                own_dp[2 * h + c, :, cols] = dprobs
                own_st[2 * h + c, 0:1, cols] = highest
                own_st[2 * h + c, 1:2, cols] = jnp.sum(weights, axis=0, keepdims=True)
                own_st[2 * h + c, 2:3, cols] = jnp.sum(weights * dprobs, axis=0, keepdims=True)

    def slot_head(h, keys, values):
        key_cols = slice(h * HD, (h + 1) * HD)
        value_cols = slice(256 + h * HD, 256 + (h + 1) * HD)
        key_sum, value_sum = 0.0, 0.0
        for c in range(2):
            live = row_at < lens[0, c]
            for g in range(0, 8, 2):
                cols = slice(g * HD, (g + 2) * HD)
                probs, dscores, own_probs, own_dscores = joined_tile(
                    keys, values, heads(aq, c, h, g, 2), heads(ag, c, h, g, 2),
                    own_w[2 * h + c, :, cols], own_dp[2 * h + c, :, cols], own_st[2 * h + c, :, cols], live,
                )
                probs_s[c, 0:128, cols] = probs
                probs_s[c, 128:256, cols] = own_probs
                dsc_s[c, 0:128, cols] = dscores
                dsc_s[c, 128:256, cols] = own_dscores
            key_grad = mm(dsc_s[c], heads(aq, c, h, 0, 8), NN) * FACTOR
            value_grad = mm(probs_s[c], heads(ag, c, h, 0, 8), NN)
            dkv[256 + c * T:256 + (c + 1) * T, key_cols] = key_grad[T:].astype(jnp.bfloat16)
            dkv[256 + c * T:256 + (c + 1) * T, value_cols] = value_grad[T:].astype(jnp.bfloat16)
            key_sum = key_sum + key_grad[:T]
            value_sum = value_sum + value_grad[:T]
        dkv[128:256, key_cols] = key_sum.astype(jnp.bfloat16)
        dkv[128:256, value_cols] = value_sum.astype(jnp.bfloat16)

    ready(got.at[pl.ds(0, 15)], recv_sem.at[2])
    from_plane = pairing[0, r] // 4
    for shift in range(3):
        for k in range(4):
            pre[4 * shift + k] = got[lax.rem(from_plane + SHIFTS[shift], 4) * 4 + k]
    slot_head(0, pre[0:4].reshape(T, HD), pre[4:8].reshape(T, HD))
    ready(got2.at[pl.ds(0, 15)], recv_sem.at[3])
    for shift in range(3):
        for k in range(4):
            pre2[4 * shift + k] = got2[lax.rem(from_plane + SHIFTS[shift], 4) * 4 + k]

    a_pre[rows(f, 64), :] = pre2[8:12].reshape(64, HD)
    a_copy = to(a_pre.at[rows(f, 64)], a_pre.at[rows(f, 64)], 5, twin)
    a_copy.start()
    slot_head(1, pre[8:12].reshape(T, HD), pre2[0:8].reshape(T, HD))

    ready(a_pre.at[pl.ds(0, 64)], recv_sem.at[5])
    a_cols[:, 0:128] = jnp.transpose(a_pre[...])
    for b, (row, col) in enumerate([(0, 0), (0, 128), (64, 256), (64, 384)]):
        block = outer_acc[row:row + 64, col:col + 128] + mm(
            a_cols[row:row + 64, :], dkv[128:512, col:col + 128], NN
        )
        gr_send[4 * b:4 * b + 4] = block.astype(jnp.bfloat16).reshape(4, 16, 128)
    for k in PLANE_ORDER:
        peer = (lax.rem(y + k // 4, 4)) * 4 + lax.rem(x + k % 4, 4)
        to(gr_send.at[peer], gr1.at[plane], 7, in_plane(peer)).start()
    gr1[plane] = gr_send[plane]

    pre_part[...] = mm(dkv[128:256, :], wide_up[...], NT)
    pre_half[0] = pre_part[rows(1 - f, 64), :].astype(jnp.bfloat16)
    pre_copy = to(pre_half.at[0], pre_twin, 6, twin)
    pre_copy.start()

    an_send[...] = mm(dkv[256:512, :], wide_up[...], NT).astype(jnp.bfloat16)
    to_twin = to(an_send, an_recv, 9, twin)

    ready(pre_twin, recv_sem.at[6])
    both = (pre_part[rows(f, 64), :] + pre_twin[...].astype(jnp.float32)).astype(jnp.bfloat16)
    pre_half[1] = both
    for k in (2, 1, 3):
        to(pre_half.at[1], pre_z.at[z_hi], 10, {"resp": along_z(k)}).start()
    pre_z[z_hi] = both
    to_twin.start()

    ready(gr1.at[pl.ds(0, 15)], recv_sem.at[7])
    part_sum = jnp.sum(gr1[...].astype(jnp.float32), axis=0).astype(jnp.bfloat16)
    gr2_send[...] = part_sum
    for k in RING_ORDER:
        to(gr2_send, gr2.at[ring], 11, in_ring(lax.rem(ring + k, N))).start()
    gr2[ring] = part_sum

    ready(an_recv, recv_sem.at[9])
    answer_out[0] = an_send[...].astype(jnp.float32) + an_recv[...].astype(jnp.float32)

    def responder(owner):
        held = jnp.int32(0)
        for d in range(N):
            held = jnp.where(pairing[0, d] == owner, d, held)
        return held

    sources = [responder(along_x(k)) for k in range(4)]
    ready(own_twin, recv_sem.at[4])
    ready(pre_z.at[pl.ds(0, 3)], recv_sem.at[10])
    for k in (2, 1, 3, 0):
        mine = pre_z[jnp.where(lax.rem(sources[k], 4) == x, sources[k] // 4, z_hi)]
        if k:
            pre_pick[k] = mine
            to(pre_pick.at[k], pre_home.at[x], 12, {"resp": along_x(k)}).start()
        else:
            pre_home[x] = mine

    ready(gr2.at[pl.ds(0, 15)], recv_sem.at[11])
    total = (jnp.sum(gr2[...].astype(jnp.float32), axis=0) * scale).astype(jnp.bfloat16)
    gr3_send[...] = total
    for k in PLANE_ORDER:
        peer = (lax.rem(y + k // 4, 4)) * 4 + lax.rem(x + k % 4, 4)
        to(gr3_send, gr3.at[plane], 13, in_plane(peer)).start()
    gr3[plane] = total

    ready(pre_home.at[pl.ds(0, 3)], recv_sem.at[12])
    done = (
        own_proj[rows(f, 64), :]
        + own_twin[...].astype(jnp.float32)
        + pre_home[lax.rem(sources[0], 4)].astype(jnp.float32)
    )
    done_half[...] = done
    done_copy = to(done_half, done_twin, 14, twin)
    done_copy.start()
    prompt_out[0, rows(f, 64), :] = done
    ready(done_twin, recv_sem.at[14])
    prompt_out[0, rows(1 - f, 64), :] = done_twin[...]

    ready(gr3.at[pl.ds(0, 15)], recv_sem.at[13])
    for b in range(4):
        up_out[b // 2, :, (b % 2) * 128:(b % 2) * 128 + 128] = (
            gr3[4 * b:4 * b + 4].reshape(64, 128).astype(jnp.float32)
        )

    ready(mid1.at[pl.ds(0, 11)], send_sem.at[0])
    ready(got.at[pl.ds(0, 15)], send_sem.at[2])
    ready(got2.at[pl.ds(0, 15)], send_sem.at[3])
    own_copy.wait_send()
    a_copy.wait_send()
    pre_copy.wait_send()
    ready(gr_send.at[pl.ds(0, 15)], send_sem.at[7])
    to_twin.wait_send()
    ready(pre_z.at[pl.ds(0, 3)], send_sem.at[10])
    ready(gr2.at[pl.ds(0, 15)], send_sem.at[11])
    ready(pre_pick.at[pl.ds(0, 3)], send_sem.at[12])
    ready(gr3.at[pl.ds(0, 15)], send_sem.at[13])
    done_copy.wait_send()


def store(a, b, c, a_out, b_out, c_out, sem):
    copies = [pltpu.make_async_copy(*pair, sem.at[i]) for i, pair in enumerate([(a, a_out), (b, b_out), (c, c_out)])]
    for copy in copies:
        copy.start()
    for copy in copies:
        copy.wait()


def on_device(scale, *args):
    bf, f32 = jnp.bfloat16, jnp.float32
    hbm = pl.BlockSpec(memory_space=pltpu.HBM)
    vmem = pl.BlockSpec(memory_space=pltpu.VMEM)
    V = pltpu.VMEM
    args = [pltpu.with_memory_space_constraint(a, pltpu.HBM) for a in args]
    held = pl.pallas_call(
        functools.partial(kernel, scale),
        out_shape=(
            jax.ShapeDtypeStruct((1, 128, 128), f32),
            jax.ShapeDtypeStruct((1, 256, 128), f32),
            jax.ShapeDtypeStruct((2, 64, 256), f32),
        ),
        in_specs=[hbm] * 13,
        out_specs=(vmem, vmem, vmem),
        scratch_shapes=[
            V((128, 2048), bf), V((128, 256), bf), V((128, 256), bf), V((128, 128), bf), V((128, 2048), bf),
            V((256, 2048), bf), V((256, 256), bf), V((256, 256), bf), V((256, 128), bf), V((256, 2048), bf),
            V((2, 64, 256), bf), pltpu.SMEM((1, 2), jnp.int32), pltpu.SMEM((1, 16), jnp.int32),
            V((128, 512), bf), V((32, 16, 128), bf), V((12, 3, 16, 128), bf), V((256, 512), bf),
            V((12, 2, 16, 128), bf), V((12, 16, 128), bf),
            V((16, 3, 16, 128), bf), V((16, 3, 16, 128), bf), V((16, 2, 16, 128), bf), V((16, 16, 128), bf), V((128, 128), bf),
            V((128, 384), bf), V((4, 128, 1024), f32), V((4, 128, 1024), f32), V((4, 8, 1024), f32),
            V((2, 256, 1024), bf), V((2, 256, 1024), bf), V((512, 512), bf), V((128, 128), f32), V((128, 512), f32),
            V((64, 128), bf), V((64, 128), bf), V((128, 128), f32), V((64, 128), bf), V((2, 64, 128), bf),
            V((4, 64, 128), bf), V((4, 64, 128), bf), V((4, 64, 128), bf),
            V((64, 128), f32), V((64, 128), f32),
            V((256, 128), bf), V((256, 128), bf),
            V((16, 16, 128), bf), V((16, 16, 128), bf), V((16, 128), bf), V((16, 16, 128), bf),
            V((16, 128), bf), V((16, 16, 128), bf),
            pltpu.SemaphoreType.DMA((13,)), pltpu.SemaphoreType.DMA((15,)), pltpu.SemaphoreType.DMA((15,)),
        ],
        compiler_params=pltpu.CompilerParams(
            collective_id=0, has_side_effects=True, vmem_limit_bytes=48 * 1024 * 1024
        ),
        name="adapter_backward",
    )(*args)
    return pl.pallas_call(
        store,
        out_shape=tuple(jax.ShapeDtypeStruct(h.shape, h.dtype) for h in held),
        in_specs=[pl.BlockSpec(memory_space=pl.ANY)] * 3,
        out_specs=(pl.BlockSpec(memory_space=pl.ANY),) * 3,
        scratch_shapes=[pltpu.SemaphoreType.DMA((3,))],
        compiler_params=pltpu.CompilerParams(vmem_limit_bytes=65136 * 1024),
        name="store",
    )(*[pltpu.with_memory_space_constraint(h, pltpu.VMEM) for h in held])


def solution(mesh):
    rows = ("prompt", "resp")
    wide = P(rows, None, "fsdp")
    whole = P(rows, None, None)
    scale = 1.0 / math.sqrt(mesh.shape["prompt"] * mesh.shape["resp"] * 2 * T)
    return jax.shard_map(
        functools.partial(on_device, scale),
        mesh=mesh,
        in_specs=(
            wide, wide, wide, whole, wide, wide, wide, wide, whole, wide,
            P(None, None, "fsdp"), P(rows, None), P("prompt", None),
        ),
        out_specs=(whole, whole, P(None, None, "fsdp")),
        check_vma=False,
    )
```

```python
import functools
import math

import jax
import jax.numpy as jnp
from jax import lax
from jax.experimental import pallas as pl
from jax.experimental.pallas import tpu as pltpu
from jax.sharding import PartitionSpec as P

MESH = pl.DeviceIdType.MESH
HD = 128
T = 128
N = 16
NT = (((1,), (1,)), ((), ()))
TN = (((0,), (0,)), ((), ()))
NN = (((1,), (0,)), ((), ()))
FACTOR = 1.0 / math.sqrt(HD)
EXP2_FACTOR = FACTOR * math.log2(math.e)
SHIFTS = (0, 1, 3)
NEAR_ORDER = ((1, 2), (2, 2), (1, 1), (2, 1), (1, 3), (2, 3), (1, 0), (2, 0), (0, 2), (0, 1), (0, 3))
RESP_ORDER = (10, 6, 14, 9, 5, 13, 11, 7, 15, 8, 4, 12, 2, 1, 3)
PLANE_ORDER = (10, 9, 11, 6, 14, 8, 2, 5, 7, 13, 15, 4, 12, 1, 3)
RING_ORDER = (8, 7, 9, 6, 10, 5, 11, 4, 12, 3, 13, 2, 14, 1, 15)


def mm(a, b, dims):
    return lax.dot_general(a, b, dims, preferred_element_type=jnp.float32)


def ready(ref, sem):
    pltpu.make_async_copy(ref, ref, sem).wait()


def backward_tile(keys, values, queries, grads, visible, live, prefix):
    scores = mm(keys, queries, NT)
    dprobs = mm(values, grads, NT)
    own = jnp.where(visible, scores[prefix:], -1e30)
    highest = jnp.max(own, axis=0, keepdims=True)
    if prefix:
        highest = jnp.maximum(highest, jnp.max(scores[:prefix], axis=0, keepdims=True))
        scores = jnp.concatenate([scores[:prefix], own], axis=0)
    else:
        scores = own
    weights = jnp.exp2((scores - highest) * EXP2_FACTOR)
    inverse = 1.0 / jnp.sum(weights, axis=0, keepdims=True)
    if live is not None:
        inverse = jnp.where(live, inverse, 0.0)
    probs = weights * inverse
    delta = jnp.sum(probs * dprobs, axis=0, keepdims=True)
    dscores = probs * (dprobs - delta)
    return probs.astype(jnp.bfloat16), dscores.astype(jnp.bfloat16)


def joined_tile(keys, values, queries, grads, own_weights, own_dprobs, own_stats, live):
    scores = mm(keys, queries, NT)
    dprobs = mm(values, grads, NT)
    own_highest, own_sum, own_dot = own_stats[0:1], own_stats[1:2], own_stats[2:3]
    highest = jnp.maximum(own_highest, jnp.max(scores, axis=0, keepdims=True))
    weights = jnp.exp2((scores - highest) * EXP2_FACTOR)
    rescale = jnp.exp2((own_highest - highest) * EXP2_FACTOR)
    total = own_sum * rescale + jnp.sum(weights, axis=0, keepdims=True)
    inverse = jnp.where(live, 1.0 / total, 0.0)
    delta = (own_dot * rescale + jnp.sum(weights * dprobs, axis=0, keepdims=True)) * inverse
    probs = weights * inverse
    own_probs = own_weights * (rescale * inverse)
    return (
        probs.astype(jnp.bfloat16),
        (probs * (dprobs - delta)).astype(jnp.bfloat16),
        own_probs.astype(jnp.bfloat16),
        (own_probs * (own_dprobs - delta)).astype(jnp.bfloat16),
    )


def kernel(
    scale,
    pq_h, pk_h, pv_h, pa_h, pg_h, aq_h, ak_h, av_h, aa_h, ag_h, up_h, lens_h, pairing_h,
    prompt_out, answer_out, up_out,
    pq, pk, pv, pa, pg, aq, ak, av, aa, ag, up, lens, pairing,
    wide_up, pack, parcel, kv_slot, pre, pre2, mid1, mid2, got, got2, a_pre, a_cols, own_w, own_dp, own_st,
    probs_s, dsc_s, dkv, own_proj, outer_acc,
    own_half, own_twin, pre_part, pre_twin, pre_half, pre_z, pre_pick, pre_home, done_half, done_twin,
    an_send, an_recv, gr_send, gr1, gr2_send, gr2, gr3_send, gr3,
    load_sem, send_sem, recv_sem,
):
    f = lax.axis_index("fsdp")
    p = lax.axis_index("prompt")
    r = lax.axis_index("resp")
    twin = {"fsdp": 1 - f}
    x, z_hi = lax.rem(r, 4), r // 4
    y, z_lo = p // 4, lax.rem(p, 4)
    plane = y * 4 + x
    ring = z_hi * 4 + z_lo

    def in_plane(at):
        return {"prompt": (at // 4) * 4 + z_lo, "resp": z_hi * 4 + lax.rem(at, 4)}

    def in_ring(at):
        return {"prompt": y * 4 + lax.rem(at, 4), "resp": (at // 4) * 4 + x}

    def along_x(k):
        return z_hi * 4 + lax.rem(x + k, 4)

    def along_z(k):
        return lax.rem(z_hi + k, 4) * 4 + x

    barrier = pltpu.get_barrier_semaphore()

    def greet(where):
        pl.semaphore_signal(barrier, inc=1, device_id=where, device_id_type=MESH)

    for shift, k in NEAR_ORDER:
        greet({"resp": lax.rem(z_hi + SHIFTS[shift], 4) * 4 + lax.rem(x + k, 4)})

    loads = [
        pltpu.make_async_copy(src.at[0] if lead else src, dst, load_sem.at[i])
        for i, (src, dst, lead) in enumerate([
            (up_h, up, False), (pa_h, pa, True), (pk_h, pk, True), (pv_h, pv, True),
            (pq_h, pq, True), (pg_h, pg, True), (aa_h, aa, True), (ak_h, ak, True),
            (av_h, av, True), (aq_h, aq, True), (ag_h, ag, True), (lens_h, lens, False), (pairing_h, pairing, False),
        ])
    ]
    for load in loads:
        load.start()

    greet(twin)
    for k in range(4, N):
        greet({"prompt": (lax.rem(y + k // 4, 4)) * 4 + z_lo, "resp": along_x(k % 4)})
    for k in range(1, 4):
        greet({"prompt": y * 4 + lax.rem(z_lo + k, 4)})

    wide_up[...] = jnp.zeros_like(wide_up)
    for load in loads[:4]:
        load.wait()
    wide_up[0:64, 0:256] = up[0]
    wide_up[64:128, 256:512] = up[1]
    lifted = mm(pa[...], wide_up[...], NN)
    for i, base in enumerate((pk, pv)):
        full = (base[...].astype(jnp.float32) + lifted[:, 256 * i:256 * i + 256]).astype(jnp.bfloat16)
        for h in range(2):
            pack[16 * i + 8 * h:16 * i + 8 * h + 8] = full[:, h * HD:(h + 1) * HD].reshape(8, 16, HD)
    for i, tiles in enumerate((0, 16, 8)):
        parcel[4 * i:4 * i + 4, 0:2] = pack[tiles:tiles + 8].reshape(4, 2, 16, HD)
    parcel[0:8, 2] = pack[24:32]
    parcel[8:12, 2] = pa[pl.ds(pl.multiple_of(f * 64, 64), 64), :].reshape(4, 16, HD)

    pl.semaphore_wait(barrier, 27)

    def to(src, dst, lane, where):
        return pltpu.make_async_remote_copy(
            src_ref=src, dst_ref=dst, send_sem=send_sem.at[lane], recv_sem=recv_sem.at[lane],
            device_id=where, device_id_type=MESH,
        )

    def rows(index, size=16):
        return pl.ds(pl.multiple_of(index * size, size), size)

    for shift, k in NEAR_ORDER:
        peer_x = lax.rem(x + k, 4)
        peer = lax.rem(z_hi + SHIFTS[shift], 4) * 4 + peer_x
        to(parcel.at[4 * shift + peer_x], mid1.at[r], 0, {"resp": peer}).start()
    mid1[r] = parcel[x]
    for k in range(4):
        mid1[lax.rem(z_hi + 2, 4) * 4 + k] = jnp.zeros((3, 16, HD), jnp.bfloat16)

    lane_at = lax.rem(lax.broadcasted_iota(jnp.int32, (T, 256), 1), T)
    visible = lax.broadcasted_iota(jnp.int32, (T, 256), 0) <= lane_at
    loads[4].wait()
    loads[5].wait()

    def own_head(h, carry):
        at = pl.multiple_of(h * HD, HD)
        keys = pack[pl.ds(8 * h, 8)].reshape(T, HD)
        values = pack[pl.ds(16 + 8 * h, 8)].reshape(T, HD)

        def heads(ref, g, count):
            return jnp.concatenate(
                [ref[:, pl.ds(pl.multiple_of(h * 1024 + (g + i) * HD, HD), HD)] for i in range(count)], axis=0
            )

        for g in range(0, 8, 2):
            probs, dscores = backward_tile(keys, values, heads(pq, g, 2), heads(pg, g, 2), visible, None, 0)
            probs_s[0, 0:128, g * HD:(g + 2) * HD] = probs
            dsc_s[0, 0:128, g * HD:(g + 2) * HD] = dscores
        dkv[0:128, pl.ds(at, HD)] = (mm(dsc_s[0, 0:128, :], heads(pq, 0, 8), NN) * FACTOR).astype(jnp.bfloat16)
        dkv[0:128, pl.ds(pl.multiple_of(256 + h * HD, HD), HD)] = mm(
            probs_s[0, 0:128, :], heads(pg, 0, 8), NN
        ).astype(jnp.bfloat16)
        return carry

    lax.fori_loop(0, 2, own_head, 0)

    loads[12].wait()
    def held_of(member):
        owner = pairing[0, member]
        return jnp.where(lax.rem(owner // 4 + 6 - z_hi, 4) == 0, r, owner)

    picks = [held_of(lax.rem(r + k, N)) for k in RESP_ORDER]
    own_pick = held_of(r)
    ready(mid1.at[pl.ds(0, 11)], recv_sem.at[0])
    for k, pick in zip(RESP_ORDER, picks):
        peer = lax.rem(r + k, N)
        mid2[peer] = mid1[pick]
        to(mid2.at[peer, pl.ds(0, 2)], got.at[r], 2, {"resp": peer}).start()
    for k in RESP_ORDER:
        peer = lax.rem(r + k, N)
        to(mid2.at[peer, 2], got2.at[r], 3, {"resp": peer}).start()
    mine = mid1[own_pick]
    got[r] = mine[0:2]
    got2[r] = mine[2]

    own_proj[...] = mm(dkv[0:128, :], wide_up[...], NT)
    own_half[...] = own_proj[rows(1 - f, 64), :].astype(jnp.bfloat16)
    own_copy = to(own_half, own_twin, 4, twin)
    own_copy.start()
    for load in loads[6:12]:
        load.wait()
    lifted_slots = mm(aa[...], wide_up[...], NN)
    kv_slot[:, 0:256] = (ak[...].astype(jnp.float32) + lifted_slots[:, 0:256]).astype(jnp.bfloat16)
    kv_slot[:, 256:512] = (av[...].astype(jnp.float32) + lifted_slots[:, 256:512]).astype(jnp.bfloat16)
    outer_acc[...] = mm(pa[...], dkv[0:128, :], TN)
    a_cols[:, 128:256] = jnp.transpose(aa[0:128, :])
    a_cols[:, 256:384] = jnp.transpose(aa[128:256, :])

    row_at = lax.rem(lax.broadcasted_iota(jnp.int32, (1, 256), 1), T)

    def heads(ref, c, h, g, count):
        return jnp.concatenate(
            [ref[c * T:(c + 1) * T, (8 * h + g + i) * HD:(8 * h + g + i + 1) * HD] for i in range(count)], axis=0
        )

    for h in range(2):
        for c in range(2):
            keys = kv_slot[c * T:(c + 1) * T, h * HD:(h + 1) * HD]
            values = kv_slot[c * T:(c + 1) * T, 256 + h * HD:256 + (h + 1) * HD]
            for g in range(0, 8, 2):
                cols = slice(g * HD, (g + 2) * HD)
                scores = jnp.where(visible, mm(keys, heads(aq, c, h, g, 2), NT), -1e30)
                dprobs = mm(values, heads(ag, c, h, g, 2), NT)
                highest = jnp.max(scores, axis=0, keepdims=True)
                weights = jnp.exp2((scores - highest) * EXP2_FACTOR)
                own_w[2 * h + c, :, cols] = weights
                own_dp[2 * h + c, :, cols] = dprobs
                own_st[2 * h + c, 0:1, cols] = highest
                own_st[2 * h + c, 1:2, cols] = jnp.sum(weights, axis=0, keepdims=True)
                own_st[2 * h + c, 2:3, cols] = jnp.sum(weights * dprobs, axis=0, keepdims=True)

    def slot_head(h, keys, values):
        key_cols = slice(h * HD, (h + 1) * HD)
        value_cols = slice(256 + h * HD, 256 + (h + 1) * HD)
        key_sum, value_sum = 0.0, 0.0
        for c in range(2):
            live = row_at < lens[0, c]
            for g in range(0, 8, 2):
                cols = slice(g * HD, (g + 2) * HD)
                probs, dscores, own_probs, own_dscores = joined_tile(
                    keys, values, heads(aq, c, h, g, 2), heads(ag, c, h, g, 2),
                    own_w[2 * h + c, :, cols], own_dp[2 * h + c, :, cols], own_st[2 * h + c, :, cols], live,
                )
                probs_s[c, 0:128, cols] = probs
                probs_s[c, 128:256, cols] = own_probs
                dsc_s[c, 0:128, cols] = dscores
                dsc_s[c, 128:256, cols] = own_dscores
            key_grad = mm(dsc_s[c], heads(aq, c, h, 0, 8), NN) * FACTOR
            value_grad = mm(probs_s[c], heads(ag, c, h, 0, 8), NN)
            dkv[256 + c * T:256 + (c + 1) * T, key_cols] = key_grad[T:].astype(jnp.bfloat16)
            dkv[256 + c * T:256 + (c + 1) * T, value_cols] = value_grad[T:].astype(jnp.bfloat16)
            key_sum = key_sum + key_grad[:T]
            value_sum = value_sum + value_grad[:T]
        dkv[128:256, key_cols] = key_sum.astype(jnp.bfloat16)
        dkv[128:256, value_cols] = value_sum.astype(jnp.bfloat16)

    ready(got.at[pl.ds(0, 15)], recv_sem.at[2])
    from_plane = pairing[0, r] // 4
    for shift in range(3):
        for k in range(4):
            pre[4 * shift + k] = got[lax.rem(from_plane + SHIFTS[shift], 4) * 4 + k]
    slot_head(0, pre[0:4].reshape(T, HD), pre[4:8].reshape(T, HD))
    ready(got2.at[pl.ds(0, 15)], recv_sem.at[3])
    for shift in range(3):
        for k in range(4):
            pre2[4 * shift + k] = got2[lax.rem(from_plane + SHIFTS[shift], 4) * 4 + k]

    a_pre[rows(f, 64), :] = pre2[8:12].reshape(64, HD)
    a_copy = to(a_pre.at[rows(f, 64)], a_pre.at[rows(f, 64)], 5, twin)
    a_copy.start()
    slot_head(1, pre[8:12].reshape(T, HD), pre2[0:8].reshape(T, HD))

    ready(a_pre.at[pl.ds(0, 64)], recv_sem.at[5])
    a_cols[:, 0:128] = jnp.transpose(a_pre[...])
    for b, (row, col) in enumerate([(0, 0), (0, 128), (64, 256), (64, 384)]):
        block = outer_acc[row:row + 64, col:col + 128] + mm(
            a_cols[row:row + 64, :], dkv[128:512, col:col + 128], NN
        )
        gr_send[4 * b:4 * b + 4] = block.astype(jnp.bfloat16).reshape(4, 16, 128)
    for k in PLANE_ORDER:
        peer = (lax.rem(y + k // 4, 4)) * 4 + lax.rem(x + k % 4, 4)
        to(gr_send.at[peer], gr1.at[plane], 7, in_plane(peer)).start()
    gr1[plane] = gr_send[plane]

    pre_part[...] = mm(dkv[128:256, :], wide_up[...], NT)
    pre_half[0] = pre_part[rows(1 - f, 64), :].astype(jnp.bfloat16)
    pre_copy = to(pre_half.at[0], pre_twin, 6, twin)
    pre_copy.start()

    an_send[...] = mm(dkv[256:512, :], wide_up[...], NT).astype(jnp.bfloat16)
    to_twin = to(an_send, an_recv, 9, twin)

    ready(pre_twin, recv_sem.at[6])
    both = (pre_part[rows(f, 64), :] + pre_twin[...].astype(jnp.float32)).astype(jnp.bfloat16)
    pre_half[1] = both
    for k in (2, 1, 3):
        to(pre_half.at[1], pre_z.at[z_hi], 10, {"resp": along_z(k)}).start()
    pre_z[z_hi] = both
    to_twin.start()

    ready(gr1.at[pl.ds(0, 15)], recv_sem.at[7])
    part_sum = jnp.sum(gr1[...].astype(jnp.float32), axis=0).astype(jnp.bfloat16)
    gr2_send[...] = part_sum
    for k in RING_ORDER:
        to(gr2_send, gr2.at[ring], 11, in_ring(lax.rem(ring + k, N))).start()
    gr2[ring] = part_sum

    ready(an_recv, recv_sem.at[9])
    answer_out[0] = an_send[...].astype(jnp.float32) + an_recv[...].astype(jnp.float32)

    def responder(owner):
        held = jnp.int32(0)
        for d in range(N):
            held = jnp.where(pairing[0, d] == owner, d, held)
        return held

    sources = [responder(along_x(k)) for k in range(4)]
    ready(own_twin, recv_sem.at[4])
    ready(pre_z.at[pl.ds(0, 3)], recv_sem.at[10])
    for k in (2, 1, 3, 0):
        mine = pre_z[jnp.where(lax.rem(sources[k], 4) == x, sources[k] // 4, z_hi)]
        if k:
            pre_pick[k] = mine
            to(pre_pick.at[k], pre_home.at[x], 12, {"resp": along_x(k)}).start()
        else:
            pre_home[x] = mine

    ready(gr2.at[pl.ds(0, 15)], recv_sem.at[11])
    total = (jnp.sum(gr2[...].astype(jnp.float32), axis=0) * scale).astype(jnp.bfloat16)
    gr3_send[...] = total
    for k in PLANE_ORDER:
        peer = (lax.rem(y + k // 4, 4)) * 4 + lax.rem(x + k % 4, 4)
        to(gr3_send, gr3.at[plane], 13, in_plane(peer)).start()
    gr3[plane] = total

    ready(pre_home.at[pl.ds(0, 3)], recv_sem.at[12])
    done = (
        own_proj[rows(f, 64), :]
        + own_twin[...].astype(jnp.float32)
        + pre_home[lax.rem(sources[0], 4)].astype(jnp.float32)
    )
    done_half[...] = done
    done_copy = to(done_half, done_twin, 14, twin)
    done_copy.start()
    prompt_out[0, rows(f, 64), :] = done
    ready(done_twin, recv_sem.at[14])
    prompt_out[0, rows(1 - f, 64), :] = done_twin[...]

    ready(gr3.at[pl.ds(0, 15)], recv_sem.at[13])
    for b in range(4):
        up_out[b // 2, :, (b % 2) * 128:(b % 2) * 128 + 128] = (
            gr3[4 * b:4 * b + 4].reshape(64, 128).astype(jnp.float32)
        )

    ready(mid1.at[pl.ds(0, 11)], send_sem.at[0])
    ready(got.at[pl.ds(0, 15)], send_sem.at[2])
    ready(got2.at[pl.ds(0, 15)], send_sem.at[3])
    own_copy.wait_send()
    a_copy.wait_send()
    pre_copy.wait_send()
    ready(gr_send.at[pl.ds(0, 15)], send_sem.at[7])
    to_twin.wait_send()
    ready(pre_z.at[pl.ds(0, 3)], send_sem.at[10])
    ready(gr2.at[pl.ds(0, 15)], send_sem.at[11])
    ready(pre_pick.at[pl.ds(0, 3)], send_sem.at[12])
    ready(gr3.at[pl.ds(0, 15)], send_sem.at[13])
    done_copy.wait_send()


def store(a, b, c, a_out, b_out, c_out, sem):
    copies = [pltpu.make_async_copy(*pair, sem.at[i]) for i, pair in enumerate([(a, a_out), (b, b_out), (c, c_out)])]
    for copy in copies:
        copy.start()
    for copy in copies:
        copy.wait()


def on_device(scale, *args):
    bf, f32 = jnp.bfloat16, jnp.float32
    hbm = pl.BlockSpec(memory_space=pltpu.HBM)
    vmem = pl.BlockSpec(memory_space=pltpu.VMEM)
    V = pltpu.VMEM
    args = [pltpu.with_memory_space_constraint(a, pltpu.HBM) for a in args]
    held = pl.pallas_call(
        functools.partial(kernel, scale),
        out_shape=(
            jax.ShapeDtypeStruct((1, 128, 128), f32),
            jax.ShapeDtypeStruct((1, 256, 128), f32),
            jax.ShapeDtypeStruct((2, 64, 256), f32),
        ),
        in_specs=[hbm] * 13,
        out_specs=(vmem, vmem, vmem),
        scratch_shapes=[
            V((128, 2048), bf), V((128, 256), bf), V((128, 256), bf), V((128, 128), bf), V((128, 2048), bf),
            V((256, 2048), bf), V((256, 256), bf), V((256, 256), bf), V((256, 128), bf), V((256, 2048), bf),
            V((2, 64, 256), bf), pltpu.SMEM((1, 2), jnp.int32), pltpu.SMEM((1, 16), jnp.int32),
            V((128, 512), bf), V((32, 16, 128), bf), V((12, 3, 16, 128), bf), V((256, 512), bf),
            V((12, 2, 16, 128), bf), V((12, 16, 128), bf),
            V((16, 3, 16, 128), bf), V((16, 3, 16, 128), bf), V((16, 2, 16, 128), bf), V((16, 16, 128), bf), V((128, 128), bf),
            V((128, 384), bf), V((4, 128, 1024), f32), V((4, 128, 1024), f32), V((4, 8, 1024), f32),
            V((2, 256, 1024), bf), V((2, 256, 1024), bf), V((512, 512), bf), V((128, 128), f32), V((128, 512), f32),
            V((64, 128), bf), V((64, 128), bf), V((128, 128), f32), V((64, 128), bf), V((2, 64, 128), bf),
            V((4, 64, 128), bf), V((4, 64, 128), bf), V((4, 64, 128), bf),
            V((64, 128), f32), V((64, 128), f32),
            V((256, 128), bf), V((256, 128), bf),
            V((16, 16, 128), bf), V((16, 16, 128), bf), V((16, 128), bf), V((16, 16, 128), bf),
            V((16, 128), bf), V((16, 16, 128), bf),
            pltpu.SemaphoreType.DMA((13,)), pltpu.SemaphoreType.DMA((15,)), pltpu.SemaphoreType.DMA((15,)),
        ],
        compiler_params=pltpu.CompilerParams(
            collective_id=0, has_side_effects=True, vmem_limit_bytes=48 * 1024 * 1024
        ),
        name="adapter_backward",
    )(*args)
    return pl.pallas_call(
        store,
        out_shape=tuple(jax.ShapeDtypeStruct(h.shape, h.dtype) for h in held),
        in_specs=[pl.BlockSpec(memory_space=pl.ANY)] * 3,
        out_specs=(pl.BlockSpec(memory_space=pl.ANY),) * 3,
        scratch_shapes=[pltpu.SemaphoreType.DMA((3,))],
        compiler_params=pltpu.CompilerParams(vmem_limit_bytes=65136 * 1024),
        name="store",
    )(*[pltpu.with_memory_space_constraint(h, pltpu.VMEM) for h in held])


def solution(mesh):
    rows = ("prompt", "resp")
    wide = P(rows, None, "fsdp")
    whole = P(rows, None, None)
    scale = 1.0 / math.sqrt(mesh.shape["prompt"] * mesh.shape["resp"] * 2 * T)
    return jax.shard_map(
        functools.partial(on_device, scale),
        mesh=mesh,
        in_specs=(
            wide, wide, wide, whole, wide, wide, wide, wide, whole, wide,
            P(None, None, "fsdp"), P(rows, None), P("prompt", None),
        ),
        out_specs=(whole, whole, P(None, None, "fsdp")),
        check_vma=False,
    )
```

```python
import functools
import math

import jax
import jax.numpy as jnp
from jax import lax
from jax.experimental import pallas as pl
from jax.experimental.pallas import tpu as pltpu
from jax.sharding import PartitionSpec as P

MESH = pl.DeviceIdType.MESH
HD = 128
T = 128
N = 16
NT = (((1,), (1,)), ((), ()))
TN = (((0,), (0,)), ((), ()))
NN = (((1,), (0,)), ((), ()))
FACTOR = 1.0 / math.sqrt(HD)
EXP2_FACTOR = FACTOR * math.log2(math.e)
SHIFTS = (0, 1, 3)
NEAR_ORDER = ((1, 2), (2, 2), (1, 1), (2, 1), (1, 3), (2, 3), (1, 0), (2, 0), (0, 2), (0, 1), (0, 3))
RESP_ORDER = (10, 6, 14, 9, 5, 13, 11, 7, 15, 8, 4, 12, 2, 1, 3)
PLANE_ORDER = (10, 9, 11, 6, 14, 8, 2, 5, 7, 13, 15, 4, 12, 1, 3)
RING_ORDER = (8, 7, 9, 6, 10, 5, 11, 4, 12, 3, 13, 2, 14, 1, 15)


def mm(a, b, dims):
    return lax.dot_general(a, b, dims, preferred_element_type=jnp.float32)


def ready(ref, sem):
    pltpu.make_async_copy(ref, ref, sem).wait()


def backward_tile(keys, values, queries, grads, visible, live, prefix):
    scores = mm(keys, queries, NT)
    dprobs = mm(values, grads, NT)
    own = jnp.where(visible, scores[prefix:], -1e30)
    highest = jnp.max(own, axis=0, keepdims=True)
    if prefix:
        highest = jnp.maximum(highest, jnp.max(scores[:prefix], axis=0, keepdims=True))
        scores = jnp.concatenate([scores[:prefix], own], axis=0)
    else:
        scores = own
    weights = jnp.exp2((scores - highest) * EXP2_FACTOR)
    inverse = 1.0 / jnp.sum(weights, axis=0, keepdims=True)
    if live is not None:
        inverse = jnp.where(live, inverse, 0.0)
    probs = weights * inverse
    delta = jnp.sum(probs * dprobs, axis=0, keepdims=True)
    dscores = probs * (dprobs - delta)
    return probs.astype(jnp.bfloat16), dscores.astype(jnp.bfloat16)


def joined_tile(keys, values, queries, grads, own_weights, own_dprobs, own_stats, live):
    scores = mm(keys, queries, NT)
    dprobs = mm(values, grads, NT)
    own_highest, own_sum, own_dot = own_stats[0:1], own_stats[1:2], own_stats[2:3]
    highest = jnp.maximum(own_highest, jnp.max(scores, axis=0, keepdims=True))
    weights = jnp.exp2((scores - highest) * EXP2_FACTOR)
    rescale = jnp.exp2((own_highest - highest) * EXP2_FACTOR)
    total = own_sum * rescale + jnp.sum(weights, axis=0, keepdims=True)
    inverse = jnp.where(live, 1.0 / total, 0.0)
    delta = (own_dot * rescale + jnp.sum(weights * dprobs, axis=0, keepdims=True)) * inverse
    probs = weights * inverse
    own_probs = own_weights * (rescale * inverse)
    return (
        probs.astype(jnp.bfloat16),
        (probs * (dprobs - delta)).astype(jnp.bfloat16),
        own_probs.astype(jnp.bfloat16),
        (own_probs * (own_dprobs - delta)).astype(jnp.bfloat16),
    )


def kernel(
    scale,
    pq_h, pk_h, pv_h, pa_h, pg_h, aq_h, ak_h, av_h, aa_h, ag_h, up_h, lens_h, pairing_h,
    prompt_out, answer_out, up_out,
    pq, pk, pv, pa, pg, aq, ak, av, aa, ag, up, lens, pairing,
    wide_up, pack, parcel, kv_slot, pre, pre2, mid1, mid1b, mid2, mid2b, got, got2, a_pre, a_cols, own_w, own_dp, own_st,
    probs_s, dsc_s, dkv, own_proj, outer_acc,
    own_half, own_twin, pre_part, pre_twin, pre_half, pre_z, pre_pick, pre_home, done_half, done_twin,
    an_send, an_recv, gr_send, gr1, gr2_send, gr2, gr3_send, gr3,
    load_sem, send_sem, recv_sem,
):
    f = lax.axis_index("fsdp")
    p = lax.axis_index("prompt")
    r = lax.axis_index("resp")
    twin = {"fsdp": 1 - f}
    x, z_hi = lax.rem(r, 4), r // 4
    y, z_lo = p // 4, lax.rem(p, 4)
    plane = y * 4 + x
    ring = z_hi * 4 + z_lo

    def in_plane(at):
        return {"prompt": (at // 4) * 4 + z_lo, "resp": z_hi * 4 + lax.rem(at, 4)}

    def in_ring(at):
        return {"prompt": y * 4 + lax.rem(at, 4), "resp": (at // 4) * 4 + x}

    def along_x(k):
        return z_hi * 4 + lax.rem(x + k, 4)

    def along_z(k):
        return lax.rem(z_hi + k, 4) * 4 + x

    barrier = pltpu.get_barrier_semaphore()

    def greet(where):
        pl.semaphore_signal(barrier, inc=1, device_id=where, device_id_type=MESH)

    for shift, k in NEAR_ORDER:
        greet({"resp": lax.rem(z_hi + SHIFTS[shift], 4) * 4 + lax.rem(x + k, 4)})

    loads = [
        pltpu.make_async_copy(src.at[0] if lead else src, dst, load_sem.at[i])
        for i, (src, dst, lead) in enumerate([
            (up_h, up, False), (pa_h, pa, True), (pk_h, pk, True), (pv_h, pv, True),
            (pq_h, pq, True), (pg_h, pg, True), (aa_h, aa, True), (ak_h, ak, True),
            (av_h, av, True), (aq_h, aq, True), (ag_h, ag, True), (lens_h, lens, False), (pairing_h, pairing, False),
        ])
    ]
    for load in loads:
        load.start()

    greet(twin)
    for k in range(4, N):
        greet({"prompt": (lax.rem(y + k // 4, 4)) * 4 + z_lo, "resp": along_x(k % 4)})
    for k in range(1, 4):
        greet({"prompt": y * 4 + lax.rem(z_lo + k, 4)})

    wide_up[...] = jnp.zeros_like(wide_up)
    for load in loads[:4]:
        load.wait()
    wide_up[0:64, 0:256] = up[0]
    wide_up[64:128, 256:512] = up[1]
    lifted = mm(pa[...], wide_up[...], NN)
    for i, base in enumerate((pk, pv)):
        full = (base[...].astype(jnp.float32) + lifted[:, 256 * i:256 * i + 256]).astype(jnp.bfloat16)
        for h in range(2):
            pack[16 * i + 8 * h:16 * i + 8 * h + 8] = full[:, h * HD:(h + 1) * HD].reshape(8, 16, HD)
    for i, tiles in enumerate((0, 16, 8)):
        parcel[4 * i:4 * i + 4, 0:2] = pack[tiles:tiles + 8].reshape(4, 2, 16, HD)
    parcel[0:8, 2] = pack[24:32]
    parcel[8:12, 2] = pa[pl.ds(pl.multiple_of(f * 64, 64), 64), :].reshape(4, 16, HD)

    pl.semaphore_wait(barrier, 27)

    def to(src, dst, lane, where):
        return pltpu.make_async_remote_copy(
            src_ref=src, dst_ref=dst, send_sem=send_sem.at[lane], recv_sem=recv_sem.at[lane],
            device_id=where, device_id_type=MESH,
        )

    def rows(index, size=16):
        return pl.ds(pl.multiple_of(index * size, size), size)

    for shift, k in NEAR_ORDER:
        peer_x = lax.rem(x + k, 4)
        peer = lax.rem(z_hi + SHIFTS[shift], 4) * 4 + peer_x
        to(parcel.at[4 * shift + peer_x, pl.ds(0, 2)], mid1.at[r], 0, {"resp": peer}).start()
    for shift, k in NEAR_ORDER:
        peer_x = lax.rem(x + k, 4)
        peer = lax.rem(z_hi + SHIFTS[shift], 4) * 4 + peer_x
        to(parcel.at[4 * shift + peer_x, 2], mid1b.at[r], 1, {"resp": peer}).start()
    mid1[r] = parcel[x, 0:2]
    mid1b[r] = parcel[x, 2]
    for k in range(4):
        mid1[lax.rem(z_hi + 2, 4) * 4 + k] = jnp.zeros((2, 16, HD), jnp.bfloat16)
        mid1b[lax.rem(z_hi + 2, 4) * 4 + k] = jnp.zeros((16, HD), jnp.bfloat16)

    lane_at = lax.rem(lax.broadcasted_iota(jnp.int32, (T, 256), 1), T)
    visible = lax.broadcasted_iota(jnp.int32, (T, 256), 0) <= lane_at
    loads[4].wait()
    loads[5].wait()

    def own_head(h, carry):
        at = pl.multiple_of(h * HD, HD)
        keys = pack[pl.ds(8 * h, 8)].reshape(T, HD)
        values = pack[pl.ds(16 + 8 * h, 8)].reshape(T, HD)

        def heads(ref, g, count):
            return jnp.concatenate(
                [ref[:, pl.ds(pl.multiple_of(h * 1024 + (g + i) * HD, HD), HD)] for i in range(count)], axis=0
            )

        for g in range(0, 8, 2):
            probs, dscores = backward_tile(keys, values, heads(pq, g, 2), heads(pg, g, 2), visible, None, 0)
            probs_s[0, 0:128, g * HD:(g + 2) * HD] = probs
            dsc_s[0, 0:128, g * HD:(g + 2) * HD] = dscores
        dkv[0:128, pl.ds(at, HD)] = (mm(dsc_s[0, 0:128, :], heads(pq, 0, 8), NN) * FACTOR).astype(jnp.bfloat16)
        dkv[0:128, pl.ds(pl.multiple_of(256 + h * HD, HD), HD)] = mm(
            probs_s[0, 0:128, :], heads(pg, 0, 8), NN
        ).astype(jnp.bfloat16)
        return carry

    lax.fori_loop(0, 2, own_head, 0)

    loads[12].wait()
    def held_of(member):
        owner = pairing[0, member]
        return jnp.where(lax.rem(owner // 4 + 6 - z_hi, 4) == 0, r, owner)

    picks = [held_of(lax.rem(r + k, N)) for k in RESP_ORDER]
    own_pick = held_of(r)
    ready(mid1.at[pl.ds(0, 11)], recv_sem.at[0])
    for k, pick in zip(RESP_ORDER, picks):
        peer = lax.rem(r + k, N)
        mid2[peer] = mid1[pick]
        to(mid2.at[peer], got.at[r], 2, {"resp": peer}).start()
    got[r] = mid1[own_pick]
    ready(mid1b.at[pl.ds(0, 11)], recv_sem.at[1])
    for k, pick in zip(RESP_ORDER, picks):
        peer = lax.rem(r + k, N)
        mid2b[peer] = mid1b[pick]
        to(mid2b.at[peer], got2.at[r], 3, {"resp": peer}).start()
    got2[r] = mid1b[own_pick]

    own_proj[...] = mm(dkv[0:128, :], wide_up[...], NT)
    own_half[...] = own_proj[rows(1 - f, 64), :].astype(jnp.bfloat16)
    own_copy = to(own_half, own_twin, 4, twin)
    own_copy.start()
    for load in loads[6:12]:
        load.wait()
    lifted_slots = mm(aa[...], wide_up[...], NN)
    kv_slot[:, 0:256] = (ak[...].astype(jnp.float32) + lifted_slots[:, 0:256]).astype(jnp.bfloat16)
    kv_slot[:, 256:512] = (av[...].astype(jnp.float32) + lifted_slots[:, 256:512]).astype(jnp.bfloat16)
    outer_acc[...] = mm(pa[...], dkv[0:128, :], TN)
    a_cols[:, 128:256] = jnp.transpose(aa[0:128, :])
    a_cols[:, 256:384] = jnp.transpose(aa[128:256, :])

    row_at = lax.rem(lax.broadcasted_iota(jnp.int32, (1, 256), 1), T)

    def heads(ref, c, h, g, count):
        return jnp.concatenate(
            [ref[c * T:(c + 1) * T, (8 * h + g + i) * HD:(8 * h + g + i + 1) * HD] for i in range(count)], axis=0
        )

    for h in range(2):
        for c in range(2):
            keys = kv_slot[c * T:(c + 1) * T, h * HD:(h + 1) * HD]
            values = kv_slot[c * T:(c + 1) * T, 256 + h * HD:256 + (h + 1) * HD]
            for g in range(0, 8, 2):
                cols = slice(g * HD, (g + 2) * HD)
                scores = jnp.where(visible, mm(keys, heads(aq, c, h, g, 2), NT), -1e30)
                dprobs = mm(values, heads(ag, c, h, g, 2), NT)
                highest = jnp.max(scores, axis=0, keepdims=True)
                weights = jnp.exp2((scores - highest) * EXP2_FACTOR)
                own_w[2 * h + c, :, cols] = weights
                own_dp[2 * h + c, :, cols] = dprobs
                own_st[2 * h + c, 0:1, cols] = highest
                own_st[2 * h + c, 1:2, cols] = jnp.sum(weights, axis=0, keepdims=True)
                own_st[2 * h + c, 2:3, cols] = jnp.sum(weights * dprobs, axis=0, keepdims=True)

    def slot_head(h, keys, values):
        key_cols = slice(h * HD, (h + 1) * HD)
        value_cols = slice(256 + h * HD, 256 + (h + 1) * HD)
        key_sum, value_sum = 0.0, 0.0
        for c in range(2):
            live = row_at < lens[0, c]
            for g in range(0, 8, 2):
                cols = slice(g * HD, (g + 2) * HD)
                probs, dscores, own_probs, own_dscores = joined_tile(
                    keys, values, heads(aq, c, h, g, 2), heads(ag, c, h, g, 2),
                    own_w[2 * h + c, :, cols], own_dp[2 * h + c, :, cols], own_st[2 * h + c, :, cols], live,
                )
                probs_s[c, 0:128, cols] = probs
                probs_s[c, 128:256, cols] = own_probs
                dsc_s[c, 0:128, cols] = dscores
                dsc_s[c, 128:256, cols] = own_dscores
            key_grad = mm(dsc_s[c], heads(aq, c, h, 0, 8), NN) * FACTOR
            value_grad = mm(probs_s[c], heads(ag, c, h, 0, 8), NN)
            dkv[256 + c * T:256 + (c + 1) * T, key_cols] = key_grad[T:].astype(jnp.bfloat16)
            dkv[256 + c * T:256 + (c + 1) * T, value_cols] = value_grad[T:].astype(jnp.bfloat16)
            key_sum = key_sum + key_grad[:T]
            value_sum = value_sum + value_grad[:T]
        dkv[128:256, key_cols] = key_sum.astype(jnp.bfloat16)
        dkv[128:256, value_cols] = value_sum.astype(jnp.bfloat16)

    ready(got.at[pl.ds(0, 15)], recv_sem.at[2])
    from_plane = pairing[0, r] // 4
    for shift in range(3):
        for k in range(4):
            pre[4 * shift + k] = got[lax.rem(from_plane + SHIFTS[shift], 4) * 4 + k]
    slot_head(0, pre[0:4].reshape(T, HD), pre[4:8].reshape(T, HD))
    ready(got2.at[pl.ds(0, 15)], recv_sem.at[3])
    for shift in range(3):
        for k in range(4):
            pre2[4 * shift + k] = got2[lax.rem(from_plane + SHIFTS[shift], 4) * 4 + k]

    a_pre[rows(f, 64), :] = pre2[8:12].reshape(64, HD)
    a_copy = to(a_pre.at[rows(f, 64)], a_pre.at[rows(f, 64)], 5, twin)
    a_copy.start()
    slot_head(1, pre[8:12].reshape(T, HD), pre2[0:8].reshape(T, HD))

    ready(a_pre.at[pl.ds(0, 64)], recv_sem.at[5])
    a_cols[:, 0:128] = jnp.transpose(a_pre[...])
    for b, (row, col) in enumerate([(0, 0), (0, 128), (64, 256), (64, 384)]):
        block = outer_acc[row:row + 64, col:col + 128] + mm(
            a_cols[row:row + 64, :], dkv[128:512, col:col + 128], NN
        )
        gr_send[4 * b:4 * b + 4] = block.astype(jnp.bfloat16).reshape(4, 16, 128)
    for k in PLANE_ORDER:
        peer = (lax.rem(y + k // 4, 4)) * 4 + lax.rem(x + k % 4, 4)
        to(gr_send.at[peer], gr1.at[plane], 7, in_plane(peer)).start()
    gr1[plane] = gr_send[plane]

    pre_part[...] = mm(dkv[128:256, :], wide_up[...], NT)
    pre_half[0] = pre_part[rows(1 - f, 64), :].astype(jnp.bfloat16)
    pre_copy = to(pre_half.at[0], pre_twin, 6, twin)
    pre_copy.start()

    an_send[...] = mm(dkv[256:512, :], wide_up[...], NT).astype(jnp.bfloat16)
    to_twin = to(an_send, an_recv, 9, twin)

    ready(pre_twin, recv_sem.at[6])
    both = (pre_part[rows(f, 64), :] + pre_twin[...].astype(jnp.float32)).astype(jnp.bfloat16)
    pre_half[1] = both
    for k in (2, 1, 3):
        to(pre_half.at[1], pre_z.at[z_hi], 10, {"resp": along_z(k)}).start()
    pre_z[z_hi] = both
    to_twin.start()

    ready(gr1.at[pl.ds(0, 15)], recv_sem.at[7])
    part_sum = jnp.sum(gr1[...].astype(jnp.float32), axis=0).astype(jnp.bfloat16)
    gr2_send[...] = part_sum
    for k in RING_ORDER:
        to(gr2_send, gr2.at[ring], 11, in_ring(lax.rem(ring + k, N))).start()
    gr2[ring] = part_sum

    ready(an_recv, recv_sem.at[9])
    answer_out[0] = an_send[...].astype(jnp.float32) + an_recv[...].astype(jnp.float32)

    def responder(owner):
        held = jnp.int32(0)
        for d in range(N):
            held = jnp.where(pairing[0, d] == owner, d, held)
        return held

    sources = [responder(along_x(k)) for k in range(4)]
    ready(own_twin, recv_sem.at[4])
    ready(pre_z.at[pl.ds(0, 3)], recv_sem.at[10])
    for k in (2, 1, 3, 0):
        mine = pre_z[jnp.where(lax.rem(sources[k], 4) == x, sources[k] // 4, z_hi)]
        if k:
            pre_pick[k] = mine
            to(pre_pick.at[k], pre_home.at[x], 12, {"resp": along_x(k)}).start()
        else:
            pre_home[x] = mine

    ready(gr2.at[pl.ds(0, 15)], recv_sem.at[11])
    total = (jnp.sum(gr2[...].astype(jnp.float32), axis=0) * scale).astype(jnp.bfloat16)
    gr3_send[...] = total
    for k in PLANE_ORDER:
        peer = (lax.rem(y + k // 4, 4)) * 4 + lax.rem(x + k % 4, 4)
        to(gr3_send, gr3.at[plane], 13, in_plane(peer)).start()
    gr3[plane] = total

    ready(pre_home.at[pl.ds(0, 3)], recv_sem.at[12])
    done = (
        own_proj[rows(f, 64), :]
        + own_twin[...].astype(jnp.float32)
        + pre_home[lax.rem(sources[0], 4)].astype(jnp.float32)
    )
    done_half[...] = done
    done_copy = to(done_half, done_twin, 14, twin)
    done_copy.start()
    prompt_out[0, rows(f, 64), :] = done
    ready(done_twin, recv_sem.at[14])
    prompt_out[0, rows(1 - f, 64), :] = done_twin[...]

    ready(gr3.at[pl.ds(0, 15)], recv_sem.at[13])
    for b in range(4):
        up_out[b // 2, :, (b % 2) * 128:(b % 2) * 128 + 128] = (
            gr3[4 * b:4 * b + 4].reshape(64, 128).astype(jnp.float32)
        )

    ready(mid1.at[pl.ds(0, 11)], send_sem.at[0])
    ready(mid1b.at[pl.ds(0, 11)], send_sem.at[1])
    ready(got.at[pl.ds(0, 15)], send_sem.at[2])
    ready(got2.at[pl.ds(0, 15)], send_sem.at[3])
    own_copy.wait_send()
    a_copy.wait_send()
    pre_copy.wait_send()
    ready(gr_send.at[pl.ds(0, 15)], send_sem.at[7])
    to_twin.wait_send()
    ready(pre_z.at[pl.ds(0, 3)], send_sem.at[10])
    ready(gr2.at[pl.ds(0, 15)], send_sem.at[11])
    ready(pre_pick.at[pl.ds(0, 3)], send_sem.at[12])
    ready(gr3.at[pl.ds(0, 15)], send_sem.at[13])
    done_copy.wait_send()


def store(a, b, c, a_out, b_out, c_out, sem):
    copies = [pltpu.make_async_copy(*pair, sem.at[i]) for i, pair in enumerate([(a, a_out), (b, b_out), (c, c_out)])]
    for copy in copies:
        copy.start()
    for copy in copies:
        copy.wait()


def on_device(scale, *args):
    bf, f32 = jnp.bfloat16, jnp.float32
    hbm = pl.BlockSpec(memory_space=pltpu.HBM)
    vmem = pl.BlockSpec(memory_space=pltpu.VMEM)
    V = pltpu.VMEM
    args = [pltpu.with_memory_space_constraint(a, pltpu.HBM) for a in args]
    held = pl.pallas_call(
        functools.partial(kernel, scale),
        out_shape=(
            jax.ShapeDtypeStruct((1, 128, 128), f32),
            jax.ShapeDtypeStruct((1, 256, 128), f32),
            jax.ShapeDtypeStruct((2, 64, 256), f32),
        ),
        in_specs=[hbm] * 13,
        out_specs=(vmem, vmem, vmem),
        scratch_shapes=[
            V((128, 2048), bf), V((128, 256), bf), V((128, 256), bf), V((128, 128), bf), V((128, 2048), bf),
            V((256, 2048), bf), V((256, 256), bf), V((256, 256), bf), V((256, 128), bf), V((256, 2048), bf),
            V((2, 64, 256), bf), pltpu.SMEM((1, 2), jnp.int32), pltpu.SMEM((1, 16), jnp.int32),
            V((128, 512), bf), V((32, 16, 128), bf), V((12, 3, 16, 128), bf), V((256, 512), bf),
            V((12, 2, 16, 128), bf), V((12, 16, 128), bf),
            V((16, 2, 16, 128), bf), V((16, 16, 128), bf), V((16, 2, 16, 128), bf), V((16, 16, 128), bf),
            V((16, 2, 16, 128), bf), V((16, 16, 128), bf), V((128, 128), bf),
            V((128, 384), bf), V((4, 128, 1024), f32), V((4, 128, 1024), f32), V((4, 8, 1024), f32),
            V((2, 256, 1024), bf), V((2, 256, 1024), bf), V((512, 512), bf), V((128, 128), f32), V((128, 512), f32),
            V((64, 128), bf), V((64, 128), bf), V((128, 128), f32), V((64, 128), bf), V((2, 64, 128), bf),
            V((4, 64, 128), bf), V((4, 64, 128), bf), V((4, 64, 128), bf),
            V((64, 128), f32), V((64, 128), f32),
            V((256, 128), bf), V((256, 128), bf),
            V((16, 16, 128), bf), V((16, 16, 128), bf), V((16, 128), bf), V((16, 16, 128), bf),
            V((16, 128), bf), V((16, 16, 128), bf),
            pltpu.SemaphoreType.DMA((13,)), pltpu.SemaphoreType.DMA((15,)), pltpu.SemaphoreType.DMA((15,)),
        ],
        compiler_params=pltpu.CompilerParams(
            collective_id=0, has_side_effects=True, vmem_limit_bytes=48 * 1024 * 1024
        ),
        name="adapter_backward",
    )(*args)
    return pl.pallas_call(
        store,
        out_shape=tuple(jax.ShapeDtypeStruct(h.shape, h.dtype) for h in held),
        in_specs=[pl.BlockSpec(memory_space=pl.ANY)] * 3,
        out_specs=(pl.BlockSpec(memory_space=pl.ANY),) * 3,
        scratch_shapes=[pltpu.SemaphoreType.DMA((3,))],
        compiler_params=pltpu.CompilerParams(vmem_limit_bytes=65136 * 1024),
        name="store",
    )(*[pltpu.with_memory_space_constraint(h, pltpu.VMEM) for h in held])


def solution(mesh):
    rows = ("prompt", "resp")
    wide = P(rows, None, "fsdp")
    whole = P(rows, None, None)
    scale = 1.0 / math.sqrt(mesh.shape["prompt"] * mesh.shape["resp"] * 2 * T)
    return jax.shard_map(
        functools.partial(on_device, scale),
        mesh=mesh,
        in_specs=(
            wide, wide, wide, whole, wide, wide, wide, wide, whole, wide,
            P(None, None, "fsdp"), P(rows, None), P("prompt", None),
        ),
        out_specs=(whole, whole, P(None, None, "fsdp")),
        check_vma=False,
    )
```
